128 devices in a mesh: head: 8 (over y, core), expert: 16 (over z, x).
Axes of the slice: x: 4, y: 4, z: 4, core: 2. Of those that a mesh axis runs over, the one named last changes fastest.
Arguments:
- attention: bfloat16 [2048, 6144], P('expert', 'head'), may hold values from -6 to 6
- out_proj: bfloat16 [6144, 6144], P('head', 'expert'), may hold values from -0.078125 to 0.078125
- residual: bfloat16 [2048, 6144], P('expert', 'head'), may hold values from -64 to 64
- norm_gain: bfloat16 [6144], P('head'), may hold values from 0.25 to 1.75
- router: float32 [6144, 4], P('head'), may hold values from -0.02734375 to 0.02734375
- routes: int32 [2048, 2], P('expert'), may hold values from 0 to 3, all different within a row; in each aligned block of 128 rows (0 to 127, 128 to 255, ...) at most 72 rows name the same one
- cotangent: bfloat16 [2048, 6144], P('expert', 'head'), may hold values from -4 to 4
- gate_weight: bfloat16 [16, 6144, 2048], P('expert', None, 'head'), may hold values from -0.078125 to 0.078125
- up_weight: bfloat16 [16, 6144, 2048], P('expert', None, 'head'), may hold values from -0.078125 to 0.078125
- down_weight: bfloat16 [16, 2048, 6144], P('expert', None, 'head'), may hold values from -0.0625 to 0.0625
Outputs:
- layer_out: float32 [2048, 6144], P('expert', 'head')
- grad_gate: bfloat16 [16, 6144, 2048], P('expert', None, 'head')
- grad_up: bfloat16 [16, 6144, 2048], P('expert', None, 'head')
- grad_down: bfloat16 [16, 2048, 6144], P('expert', None, 'head')
The draws below stay inside these ranges and needn't reach their ends.
Inputs may be any that keep to these rules, and one draw needn't show every extreme that they name: `routes`: each row names two different experts. In each aligned block of 128 rows (the rows of one index of expert) no expert is named by more than 72 rows, and in some block one expert is named by exactly 72 rows.
All inputs are finite; a program needn't handle non-finite values.
Results may differ from the reference program's by a relative error of at most 0.025.
Values may be sent and summed in bfloat16 or wider, within the bound.
A program may use at most 128 MiB of HBM per device.

```python
import math
import jax
import jax.numpy as jnp
import numpy as np
from jax import lax

D = 6144
HEADS = 48
HEAD_DIM = 128
FF = 8192
EXPERTS = 4
TOK_DEV = 128
TOKENS = 2048
CAP = 72
GROUP = 4
FFG = 2048
N_HEAD = 8
N_EXPERT = 16


def draw_residual(key, part):
    key_base, key_rows, key_cols = jax.random.split(key, 3)
    column = jnp.arange(D, dtype=jnp.float32) / D
    base = jnp.clip(jax.random.normal(key_base, (TOKENS, D), jnp.float32), -6.0, 6.0)
    rising = jnp.sqrt(1.0 + 2.0 * column)
    row_scale = jnp.exp(jax.random.uniform(key_rows, (TOKENS, 1), jnp.float32, -1.6, 0.7))
    col_scale = jnp.exp(jax.random.uniform(key_cols, (1, D), jnp.float32, -0.7, 0.7))
    return (base * row_scale * col_scale * rising[None, :]).astype(jnp.bfloat16)


def levels(key, dims, cuts, least, largest):
    level, own = 1.0, jax.random.fold_in(key, 6)
    for dim, shards_of in cuts:
        draws = jnp.exp(jax.random.uniform(jax.random.fold_in(own, dim), (shards_of,), jnp.float32, least / len(cuts), largest / len(cuts)))
        level = level * jnp.repeat(draws, dims[dim] // shards_of).reshape([-1 if axis == dim else 1 for axis in range(len(dims))])
    return level


def deal_out(own_key, own, number, rows, count, top, reach, slope):
    order = jax.random.permutation(own_key, count)
    heavy_load, ordinary = load_shares(count, rows * top, reach, slope, True), load_shares(count, rows * top, reach, slope, False)
    places = jnp.arange(count)

    def named(lengths, offset_by):
        used = int((lengths > 0).sum())
        fixed = max(1, used // 4)
        passed = fixed + (places - fixed + offset_by * (used - fixed)) % max(1, count - fixed)
        return jnp.zeros((count,), jnp.int32).at[order[jnp.where(places < fixed, places, passed)]].set(jnp.asarray(lengths, jnp.int32))

    lengths = jnp.where(number % 4 == 0, named(heavy_load, number // 4), named(ordinary, number - number // 4 - 1))
    mixed = jax.random.permutation(jax.random.fold_in(own, 3), count)
    source_of, sink = mixed[0:count // 2 * 2:2], mixed[1:count // 2 * 2:2]
    margin = jnp.minimum(lengths[source_of] - 1, reach - lengths[sink]) // 2
    margin = jnp.where((source_of == order[0]) | (sink == order[0]) | (lengths[sink] == 0), 0, jnp.maximum(margin, 0))
    passed = jax.random.randint(jax.random.fold_in(own, 4), (count // 2,), 0, 1 << 20) % (margin + 1)
    lengths = lengths.at[source_of].add(-passed).at[sink].add(passed)
    items = jnp.searchsorted(jnp.cumsum(lengths), jnp.arange(rows * top), side="right").astype(jnp.int32)
    table = items.reshape(top, rows).T
    table = table[jax.random.permutation(jax.random.fold_in(own, 1), rows)]
    offset_by = jax.random.randint(jax.random.fold_in(own, 2), (rows, 1), 0, top)
    return jnp.take_along_axis(table, (jnp.arange(top)[None, :] + offset_by) % top, axis=1)


def load_shares(number_of, total, most, lean, full):
    loads = [(1 << 20) // math.isqrt(grade ** lean) + 1 for grade in range(1, number_of + 1)]
    largest = most if full else min(most, max(-(-total // number_of), total * loads[0] // sum(loads)))
    least = 1 if total - largest >= number_of - 1 else 0
    holding, surplus = [largest] + [least] * (number_of - 1), total - largest - least * (number_of - 1)
    while surplus > 0:
        movable = [i for i in range(1, number_of) if holding[i] < largest] or [i for i in range(1, number_of) if holding[i] < most]
        mass, budget = sum([loads[i] for i in movable]), surplus
        for i in movable:
            addition = min(most - holding[i], max(1, budget * loads[i] // mass), surplus)
            holding[i] = holding[i] + addition
            surplus = surplus - addition
    return np.array(holding)


def bell_draw(own_key, extent, scale, bound, cuts=(), kind=jnp.bfloat16):
    level = levels(own_key, extent, cuts, -0.22, 0.18) if cuts else 1.0
    values = jax.random.normal(own_key, extent, jnp.float32) * scale * level
    return jnp.minimum(jnp.maximum(values, -bound), bound).astype(kind)


def setup_inputs(seed: int = 0) -> dict:
    key_of = jax.random.split(jax.random.key(seed), 11)
    attention = bell_draw(key_of[0], (TOKENS, HEADS * HEAD_DIM), 1.0, 6.0, ((0, 16), (1, 8)))
    out_proj = bell_draw(key_of[1], (HEADS * HEAD_DIM, D), (HEADS * HEAD_DIM) ** -0.5, 0.078125, ((0, 8), (1, 16)))
    residual = draw_residual(jax.random.fold_in(key_of[10], 71), 0)
    norm_gain = jnp.clip(1.0 + 0.15 * jax.random.normal(key_of[3], (D,), jnp.float32), 0.25, 1.75).astype(jnp.bfloat16)
    router = bell_draw(key_of[4], (D, EXPERTS), (8 * D) ** -0.5, 0.02734375, ((0, 8),), jnp.float32)
    routes_keys = jax.random.split(jax.random.fold_in(key_of[5], 1), TOKENS // TOK_DEV)
    routes_turns = jax.random.permutation(jax.random.fold_in(key_of[5], 3), TOKENS // TOK_DEV)
    routes = jax.vmap(lambda own, number: deal_out(jax.random.fold_in(key_of[5], 2), own, number, TOK_DEV, EXPERTS, 2, CAP, 2))(routes_keys, routes_turns).reshape((TOKENS, 2))
    cotangent = bell_draw(key_of[6], (TOKENS, D), 0.25, 4.0, ((0, 16), (1, 8)))
    gate_weight = bell_draw(key_of[7], (N_EXPERT, D, FFG), D ** -0.5, 0.078125, ((0, 16), (2, 8)))
    up_weight = bell_draw(key_of[8], (N_EXPERT, D, FFG), D ** -0.5, 0.078125, ((0, 16), (2, 8)))
    down_weight = bell_draw(key_of[9], (N_EXPERT, FFG, D), FF ** -0.5, 0.0625, ((0, 16), (2, 8)))
    return dict(attention=attention, out_proj=out_proj, residual=residual, norm_gain=norm_gain, router=router, routes=routes, cotangent=cotangent, gate_weight=gate_weight, up_weight=up_weight, down_weight=down_weight)


EPSILON = 1e-05

def reference(attention, out_proj, residual, norm_gain, router, routes, cotangent, gate_weight, up_weight, down_weight):
    proj = jnp.dot(attention, out_proj, preferred_element_type=jnp.float32)
    state = residual.astype(jnp.float32) + proj
    scaled = state * norm_gain.astype(jnp.float32)
    inverse = lax.rsqrt(lax.optimization_barrier(jnp.mean(state * state, axis=1, keepdims=True)) + EPSILON)
    normed = (scaled * inverse).astype(jnp.bfloat16)
    logits = inverse * jnp.dot(scaled, router, precision=lax.Precision.HIGHEST, preferred_element_type=jnp.float32)
    expert_ids = jnp.arange(EXPERTS, dtype=jnp.int32)
    first_id = routes[:, 0]
    second = routes[:, 1]
    logit_first = lax.optimization_barrier(jnp.sum(jnp.where(first_id[:, None] == expert_ids[None, :], logits, 0.0), axis=1, keepdims=True))
    logit_second = lax.optimization_barrier(jnp.sum(jnp.where(second[:, None] == expert_ids[None, :], logits, 0.0), axis=1, keepdims=True))
    prob_first = jax.nn.sigmoid(logit_first - logit_second)
    prob_second = jax.nn.sigmoid(logit_second - logit_first)
    hit_table = (routes.reshape(N_EXPERT, TOK_DEV * 2)[:, :, None] == expert_ids[None, None, :]).astype(jnp.int32)
    earlier = jnp.cumsum(hit_table, axis=1, dtype=jnp.int32) - hit_table
    slot_pair = lax.optimization_barrier(jnp.sum(earlier * hit_table, axis=2, dtype=jnp.int32)).reshape(TOKENS, 2)
    source = (jnp.arange(TOKENS, dtype=jnp.int32) // TOK_DEV).astype(jnp.int32)
    position = (source[:, None] * CAP + slot_pair).astype(jnp.int32)
    rows_total = N_EXPERT * CAP
    cot_first = (prob_first * cotangent.astype(jnp.float32)).astype(jnp.bfloat16)
    cot_second = (prob_second * cotangent.astype(jnp.float32)).astype(jnp.bfloat16)
    feature_block = D // N_HEAD
    contract_rows = (((0,), (0,)), ((), ()))
    output = state
    gate_list = []
    up_list = []
    down_list = []
    for expert in range(EXPERTS):
        is_first = first_id == expert
        is_second = second == expert
        index_first = jnp.where(is_first, position[:, 0], rows_total).astype(jnp.int32)
        index_second = jnp.where(is_second, position[:, 1], rows_total).astype(jnp.int32)
        x_rows = jnp.zeros((rows_total, D), jnp.bfloat16).at[index_first].set(normed, mode='drop').at[index_second].set(normed, mode='drop')
        cot_rows = jnp.zeros((rows_total, D), jnp.bfloat16).at[index_first].set(cot_first, mode='drop').at[index_second].set(cot_second, mode='drop')
        gate_w = jnp.transpose(gate_weight[expert * GROUP:(expert + 1) * GROUP], (1, 0, 2)).reshape(D, FF)
        up_w = jnp.transpose(up_weight[expert * GROUP:(expert + 1) * GROUP], (1, 0, 2)).reshape(D, FF)
        down_w = down_weight[expert * GROUP:(expert + 1) * GROUP].reshape(FF, D)
        gate_val = jnp.dot(x_rows, gate_w, preferred_element_type=jnp.float32)
        up_val = jnp.dot(x_rows, up_w, preferred_element_type=jnp.float32)
        act_gate = jax.nn.silu(gate_val)
        hidden = (act_gate * up_val).astype(jnp.bfloat16)
        out_rows = jnp.dot(hidden, down_w, preferred_element_type=jnp.float32).astype(jnp.bfloat16)
        took_first = jnp.take(out_rows, jnp.minimum(index_first, rows_total - 1), axis=0).astype(jnp.float32)
        took_second = jnp.take(out_rows, jnp.minimum(index_second, rows_total - 1), axis=0).astype(jnp.float32)
        output = output + jnp.where(is_first[:, None], prob_first * took_first, 0.0)
        output = output + jnp.where(is_second[:, None], prob_second * took_second, 0.0)
        grad_down_e = lax.dot_general(hidden, cot_rows, contract_rows, preferred_element_type=jnp.float32).astype(jnp.bfloat16)
        hidden_grad = jnp.zeros((rows_total, FF), jnp.float32)
        for block in range(N_HEAD):
            cot_cols = cot_rows[:, block * feature_block:(block + 1) * feature_block]
            down_cols = down_w[:, block * feature_block:(block + 1) * feature_block]
            term = lax.dot_general(cot_cols, down_cols, (((1,), (1,)), ((), ())), preferred_element_type=jnp.float32).astype(jnp.bfloat16)
            term = lax.optimization_barrier(term)
            hidden_grad = hidden_grad + term.astype(jnp.float32)
        gate_sigmoid = jax.nn.sigmoid(gate_val)
        gate_grad = (hidden_grad * up_val * gate_sigmoid * (1.0 + gate_val * (1.0 - gate_sigmoid))).astype(jnp.bfloat16)
        up_grad = (hidden_grad * act_gate).astype(jnp.bfloat16)
        grad_gate_e = lax.dot_general(x_rows, gate_grad, contract_rows, preferred_element_type=jnp.float32).astype(jnp.bfloat16)
        grad_up_e = lax.dot_general(x_rows, up_grad, contract_rows, preferred_element_type=jnp.float32).astype(jnp.bfloat16)
        gate_list.append(jnp.transpose(grad_gate_e.reshape(D, GROUP, FFG), (1, 0, 2)))
        up_list.append(jnp.transpose(grad_up_e.reshape(D, GROUP, FFG), (1, 0, 2)))
        down_list.append(grad_down_e.reshape(GROUP, FFG, D))
    return (output, jnp.concatenate(gate_list, axis=0), jnp.concatenate(up_list, axis=0), jnp.concatenate(down_list, axis=0))
```

```python
import functools

import jax
import jax.numpy as jnp
from jax import lax
from jax.experimental import pallas as pl
from jax.experimental.pallas import tpu as pltpu
from jax.sharding import PartitionSpec as P

EPSILON = 1e-05
MESH = pl.DeviceIdType.MESH
BF = jnp.bfloat16
F32 = jnp.float32
MIB = 2**20


def coords():
    e, h = lax.axis_index("expert"), lax.axis_index("head")
    return e % 4, h // 2, e // 4, h % 2


def dev(x, y, z, c):
    return {"expert": z * 4 + x, "head": 2 * y + c}


def rot(i, k):
    return lax.rem(i + (k + 4), 4)


def contract(a, b, ca, cb, **kw):
    return lax.dot_general(
        a, b, (((ca,), (cb,)), ((), ())), preferred_element_type=F32, **kw
    )


class Net:
    def __init__(self, ssem, rsem, mate):
        self.ssem, self.rsem, self.mate = ssem, rsem, mate
        self.n, self.sent = 0, []

    def send(self, src, dst, to):
        tag = self.n
        self.n += 1
        copy = pltpu.make_async_remote_copy(
            src_ref=src,
            dst_ref=dst,
            send_sem=self.ssem.at[tag],
            recv_sem=self.rsem.at[tag],
            device_id=to,
            device_id_type=MESH,
        )
        copy.start()
        self.sent.append(copy)
        return tag

    def wait(self, tag, dst):
        pltpu.make_async_remote_copy(
            src_ref=dst,
            dst_ref=dst,
            send_sem=self.ssem.at[tag],
            recv_sem=self.rsem.at[tag],
            device_id=self.mate,
            device_id_type=MESH,
        ).wait_recv()

    def drain(self):
        for copy in self.sent:
            copy.wait_send()
        self.sent = []


class Gather:
    def __init__(self, net, at, a, b, to_a, to_b, lo, hi, share):
        self.net, self.at, self.a, self.b = net, at, a, b
        self.to_a, self.to_b, self.lo, self.hi, self.share = to_a, to_b, lo, hi, share
        self.t = {}

    def ref(self, ka, kb):
        return self.at(rot(self.a, ka), rot(self.b, kb))

    def along_b(self, ka):
        r = self.ref(ka, 0)
        self.t[ka, -1] = self.net.send(r, r, self.to_b(1))
        self.t[ka, 1] = self.net.send(r, r, self.to_b(-1))

    def begin(self):
        r = self.ref(0, 0)
        self.t["a", -1] = self.net.send(r, r, self.to_a(1))
        self.t["a", 1] = self.net.send(r, r, self.to_a(-1))
        self.along_b(0)
        self.share(0, 0)

    def near_a(self):
        for k, part in ((-1, self.lo), (1, self.hi)):
            r = self.ref(k, 0)
            self.net.wait(self.t["a", k], r)
            self.t["f", k] = self.net.send(r.at[part], r.at[part], self.to_a(-k))
            self.along_b(k)
            self.share(k, 0)

    def far_a(self):
        r = self.ref(2, 0)
        self.net.wait(self.t["f", -1], r.at[self.lo])
        self.net.wait(self.t["f", 1], r.at[self.hi])
        self.along_b(2)
        self.share(2, 0)

    def near_b(self, ka):
        for k, part in ((-1, self.lo), (1, self.hi)):
            r = self.ref(ka, k)
            self.net.wait(self.t[ka, k], r)
            self.t["f", ka, k] = self.net.send(r.at[part], r.at[part], self.to_b(-k))
            self.share(ka, k)

    def far_b(self, ka):
        r = self.ref(ka, 2)
        self.net.wait(self.t["f", ka, -1], r.at[self.lo])
        self.net.wait(self.t["f", ka, 1], r.at[self.hi])
        self.share(ka, 2)


def greet(devices, extra=()):
    barrier = pltpu.get_barrier_semaphore()
    for d in devices:
        pl.semaphore_signal(barrier, inc=1, device_id=d, device_id_type=MESH)
    count = len(devices)
    for d, mine in extra:

        @pl.when(jnp.logical_not(mine))
        def _(d=d):
            pl.semaphore_signal(barrier, inc=1, device_id=d, device_id_type=MESH)

        count = count + jnp.where(mine, 0, 1)
    pl.semaphore_wait(barrier, count)


def slot_masks(rts_ref, capacity):
    r0, r1 = rts_ref[0:1, :], rts_ref[1:2, :]
    n = r0.shape[1]
    ids = lax.broadcasted_iota(jnp.int32, (8, n), 0)
    hits = ((r0 == ids) | (r1 == ids)).astype(F32).astype(BF)
    before = (
        lax.broadcasted_iota(jnp.int32, (n, n), 0)
        < lax.broadcasted_iota(jnp.int32, (n, n), 1)
    ).astype(F32).astype(BF)
    earlier = contract(hits, before, 1, 0)
    slot0 = jnp.sum(jnp.where(r0 == ids, earlier, 0.0), axis=0, keepdims=True)
    slot1 = jnp.sum(jnp.where(r1 == ids, earlier, 0.0), axis=0, keepdims=True)
    rows = lax.broadcasted_iota(jnp.int32, (capacity, n), 0)
    slot0, slot1 = slot0.astype(jnp.int32), slot1.astype(jnp.int32)
    return [
        ((r0 == e) & (slot0 == rows), (r1 == e) & (slot1 == rows)) for e in range(4)
    ]


def as_column(row):
    n = row.shape[1]
    eye = lax.broadcasted_iota(jnp.int32, (n, n), 0) == lax.broadcasted_iota(
        jnp.int32, (n, n), 1
    )
    return jnp.sum(jnp.where(eye, row, 0.0), axis=1, keepdims=True)


def front_kernel(
    att, op, res, gain, rt, rts, cot,
    state_o, xs_o, cs_o, pr_o,
    attb, own, sib16, sibr, r1, fin, st2, tot16, projr, stat, xrow, crow, xr, cr,
    ssem, rsem, lsem,
):
    x, y, z, c = coords()
    h = lax.axis_index("head")
    mate = dev(x, y, z, 1 - c)
    net = Net(ssem, rsem, mate)
    turn = [(dev(2 * c + j, z, y, x // 2), (x == 2 * c + j) & (y == z) & (c == x // 2)) for j in range(2)]
    group = [
        {"expert": lax.axis_index("expert"), "head": lax.rem(h + k, 8)}
        for k in range(1, 8)
    ]
    greet(
        [dev(rot(x, 1), y, z, c), dev(rot(x, -1), y, z, c)]
        + [dev(x, y, rot(z, k), c) for k in (1, 2, 3)]
        + group,
        turn,
    )
    attb[z, x] = att[...].reshape(attb.shape[2:])

    def quiet(ka, kb):
        pass

    lo, hi = pl.ds(0, 32), pl.ds(32, 32)
    g0 = Gather(net, lambda a, b: attb.at[b, a, 0], x, z, lambda k: dev(rot(x, k), y, z, c), lambda k: dev(x, y, rot(z, k), c), lo, hi, quiet)
    g1 = Gather(net, lambda a, b: attb.at[a, b, 1], z, x, lambda k: dev(x, y, rot(z, k), c), lambda k: dev(rot(x, k), y, z, c), lo, hi, quiet)
    flows = (g0, g1)
    for g in flows:
        g.begin()
    capacity = xrow.shape[1]
    masks = slot_masks(rts, capacity)
    for e, (m0, m1) in enumerate(masks):
        pick = (m0 | m1).astype(F32).astype(BF)
        crow[e] = contract(pick, cot[...], 1, 0).astype(BF)
    for g in flows:
        g.near_a()
    for g in flows:
        g.near_b(0)
    for g in flows:
        g.far_a()
    for k in (-1, 1):
        for g in flows:
            g.near_b(k)
    for k in (0, -1):
        for g in flows:
            g.far_b(k)
    for g in flows:
        g.near_b(2)
    for k in (1, 2):
        for g in flows:
            g.far_b(k)

    def product(yy, cc):
        rows = attb[yy, pl.ds(2 * cc, 2)].reshape(256, att.shape[1])
        return contract(rows, op[...], 1, 0)

    tags = {}
    for k in (2, -1, 1, 0):
        yy = rot(y, k)
        sib16[yy] = product(yy, 1 - c).astype(BF)
        tags[k] = net.send(sib16.at[yy], sibr.at[yy], mate)
    for k in (2, -1, 1, 0):
        yy = rot(y, k)
        own[yy] = product(yy, c)
    for k in (2, -1, 1, 0):
        yy = rot(y, k)
        net.wait(tags[k], sibr.at[yy])
        own[yy] += sibr[yy].astype(F32)
        if k == 2:
            st2[0] = own[yy].astype(BF)
            ta = net.send(st2.at[0, pl.ds(0, 128)], r1.at[0], dev(x, rot(y, 1), z, c))
            tb = net.send(
                st2.at[0, pl.ds(128, 128)], r1.at[1], dev(x, rot(y, -1), z, c)
            )
    net.wait(ta, r1.at[0])
    yy = rot(y, 1)
    own[yy, 0:128, :] += r1[0].astype(F32)
    st2[1] = own[yy].astype(BF)
    tc = net.send(st2.at[1], fin.at[0], dev(x, yy, z, c))
    net.wait(tb, r1.at[1])
    yy = rot(y, -1)
    own[yy, 128:256, :] += r1[1].astype(F32)
    st2[2] = own[yy].astype(BF)
    td = net.send(st2.at[2], fin.at[1], dev(x, yy, z, c))
    net.wait(tc, fin.at[0])
    net.wait(td, fin.at[1])
    total = own[y] + fin[0].astype(F32) + fin[1].astype(F32)
    tot16[...] = total.reshape(tot16.shape).astype(BF)

    base = net.n
    net.n += 2
    i = x % 2
    for j, (d, mine) in enumerate(turn):

        def remote(j=j, d=d):
            return pltpu.make_async_remote_copy(
                src_ref=tot16.at[j],
                dst_ref=projr.at[i],
                send_sem=ssem.at[base + j],
                recv_sem=rsem.at[base + i],
                device_id=d,
                device_id_type=MESH,
            )

        @pl.when(mine)
        def _(j=j):
            pltpu.make_async_copy(tot16.at[j], projr.at[i], lsem.at[0]).start()

        @pl.when(jnp.logical_not(mine))
        def _(remote=remote):
            remote().start()

    for k in range(2):
        local = (x == 2 * c + k) & (y == z) & (c == x // 2)

        @pl.when(local)
        def _(k=k):
            pltpu.make_async_copy(tot16.at[0], projr.at[k], lsem.at[0]).wait()

        @pl.when(jnp.logical_not(local))
        def _(k=k):
            net.wait(base + k, projr.at[k])

    for j, (d, mine) in enumerate(turn):

        @pl.when(jnp.logical_not(mine))
        def _(j=j, d=d):
            pltpu.make_async_remote_copy(
                src_ref=tot16.at[j],
                dst_ref=projr.at[i],
                send_sem=ssem.at[base + j],
                recv_sem=rsem.at[base + i],
                device_id=d,
                device_id_type=MESH,
            ).wait_send()

    half = projr.shape[2]
    for k in range(2):
        cols = slice(k * half, (k + 1) * half)
        state_o[:, cols] = res[:, cols].astype(F32) + projr[k].astype(F32)
    state = state_o[...]
    scaled = state * gain[...].astype(F32)
    stat[h, 0:4, :] = contract(rt[...], scaled, 1, 1, precision=lax.Precision.HIGHEST)
    ones = jnp.ones((8, state.shape[1]), F32)
    squares = contract(ones, state * state, 1, 1, precision=lax.Precision.HIGHEST)
    stat[h, 4:8, :] = squares[0:4]
    tags = [net.send(stat.at[h], stat.at[h], d) for d in group]
    for k, tag in enumerate(tags):
        net.wait(tag, stat.at[lax.rem(h + 7 - k, 8)])
    sums = stat[0]
    for k in range(1, 8):
        sums = sums + stat[k]
    width = 8.0 * state.shape[1]
    inverse = lax.rsqrt(sums[4:5] / width + EPSILON)
    logits = sums[0:4] * inverse
    ids = lax.broadcasted_iota(jnp.int32, logits.shape, 0)
    l0 = jnp.sum(jnp.where(rts[0:1, :] == ids, logits, 0.0), axis=0, keepdims=True)
    l1 = jnp.sum(jnp.where(rts[1:2, :] == ids, logits, 0.0), axis=0, keepdims=True)
    p0, p1 = jax.nn.sigmoid(l0 - l1), jax.nn.sigmoid(l1 - l0)
    pr_o[0:1, :] = p0
    pr_o[1:2, :] = p1
    normed = (scaled * as_column(inverse)).astype(BF)
    for e, (m0, m1) in enumerate(masks):
        pick = (m0 | m1).astype(F32).astype(BF)
        xrow[e] = contract(pick, normed, 1, 0).astype(BF)
    moved = []
    for k in (1, 2, 3):
        e = rot(z, k)
        tag = net.send(xrow.at[e], xr.at[z], dev(x, y, e, c))
        moved.append((tag, xr.at[rot(z, -k)]))
    for e, (m0, m1) in enumerate(masks):
        share = jnp.sum(
            jnp.where(m0, p0, 0.0) + jnp.where(m1, p1, 0.0), axis=1, keepdims=True
        )
        crow[e] = (crow[e].astype(F32) * share).astype(BF)
    for k in (1, 2, 3):
        e = rot(z, k)
        tag = net.send(crow.at[e], cr.at[z], dev(x, y, e, c))
        moved.append((tag, cr.at[rot(z, -k)]))
    xr[z] = xrow[z]
    cr[z] = crow[z]
    for tag, ref in moved:
        net.wait(tag, ref)
    xs_o[...] = xr[...]
    cs_o[...] = cr[...]
    net.drain()


def front(attention, out_proj, residual, norm_gain, router, routes, cotangent):
    vmem = pl.BlockSpec(memory_space=pltpu.VMEM)
    rows, cols = attention.shape
    width = out_proj.shape[1]
    cap = rows * 9 // 16
    sds = jax.ShapeDtypeStruct
    return pl.pallas_call(
        front_kernel,
        out_shape=(
            sds((rows, cols), F32),
            sds((4, cap, cols), BF),
            sds((4, cap, cols), BF),
            sds((8, rows), F32),
        ),
        in_specs=[vmem] * 7,
        out_specs=(vmem,) * 4,
        scratch_shapes=[
            pltpu.VMEM((4, 4, 2, rows // 2, cols), BF),
            pltpu.VMEM((4, 2 * rows, width), F32),
            pltpu.VMEM((4, 2 * rows, width), BF),
            pltpu.VMEM((4, 2 * rows, width), BF),
            pltpu.VMEM((2, rows, width), BF),
            pltpu.VMEM((2, 2 * rows, width), BF),
            pltpu.VMEM((3, 2 * rows, width), BF),
            pltpu.VMEM((2, rows, width), BF),
            pltpu.VMEM((2, rows, width), BF),
            pltpu.VMEM((8, 8, rows), F32),
            pltpu.VMEM((4, cap, cols), BF),
            pltpu.VMEM((4, cap, cols), BF),
            pltpu.VMEM((4, cap, cols), BF),
            pltpu.VMEM((4, cap, cols), BF),
            pltpu.SemaphoreType.DMA((64,)),
            pltpu.SemaphoreType.DMA((64,)),
            pltpu.SemaphoreType.DMA((1,)),
        ],
        compiler_params=pltpu.CompilerParams(
            collective_id=0, has_side_effects=True, vmem_limit_bytes=40 * MIB
        ),
        cost_estimate=pl.CostEstimate(
            flops=3_000_000_000, bytes_accessed=4_000_000, transcendentals=0
        ),
    )(
        attention,
        out_proj,
        residual,
        norm_gain[None, :],
        router.T,
        routes.T,
        cotangent,
    )


def shards(attention, out_proj, residual, norm_gain, router, routes, cotangent, gate_weight, up_weight, down_weight):
    state, xs, cs, pr = front(attention, out_proj, residual, norm_gain, router, routes, cotangent)
    groups = [[4 * z + x for x in range(4)] for z in range(4)]
    xg = lax.all_gather(xs, "expert", axis=0, tiled=True, axis_index_groups=groups)
    cg = lax.all_gather(cs, "expert", axis=0, tiled=True, axis_index_groups=groups)
    x_rows = lax.all_gather(xg, "head", axis=2, tiled=True).reshape(1152, 6144)
    cot_rows = cg.reshape(1152, 768)
    gate_w = gate_weight[0]; up_w = up_weight[0]; down_w = down_weight[0]
    g = contract(x_rows, gate_w, 1, 0); u = contract(x_rows, up_w, 1, 0)
    act = jax.nn.silu(g)
    hid = (act * u).astype(BF)
    hid_all = lax.all_gather(hid, "head", axis=1, tiled=True)
    yp = contract(hid_all, down_w, 1, 0).astype(BF)
    yp = yp.reshape(4, 4, 72, 768).transpose(1, 0, 2, 3).reshape(16, 72, 768)
    ret = lax.all_to_all(yp, "expert", split_axis=0, concat_axis=0, tiled=True).astype(F32)
    slot_out = jnp.sum(ret.reshape(4, 4, 72, 768), axis=1).astype(BF).reshape(288, 768)
    grad_down = contract(hid_all, cot_rows, 0, 0).astype(BF)
    dh = lax.psum_scatter(contract(cot_rows, down_w, 1, 1).astype(BF), "head", scatter_dimension=1, tiled=True).astype(F32)
    s = jax.nn.sigmoid(g)
    da = (dh * u * s * (1.0 + g * (1.0 - s))).astype(BF)
    db = (dh * act).astype(BF)
    gg = contract(x_rows, da, 0, 0).astype(BF); gu = contract(x_rows, db, 0, 0).astype(BF)
    r0, r1 = routes[:, 0], routes[:, 1]
    ids = jnp.arange(4)
    hits = ((r0[:, None] == ids) | (r1[:, None] == ids)).astype(F32)
    earlier = jnp.dot(jnp.tril(jnp.ones((128, 128), F32), -1), hits)
    s0 = jnp.sum(jnp.where(r0[:, None] == ids, earlier, 0), axis=1).astype(jnp.int32) + r0 * 72
    s1 = jnp.sum(jnp.where(r1[:, None] == ids, earlier, 0), axis=1).astype(jnp.int32) + r1 * 72
    rid = jnp.arange(288)
    t0 = jnp.dot((s0[:, None] == rid).astype(BF), slot_out, preferred_element_type=F32)
    t1 = jnp.dot((s1[:, None] == rid).astype(BF), slot_out, preferred_element_type=F32)
    out = state + pr[0][:, None] * t0 + pr[1][:, None] * t1
    return out, gg[None], gu[None], grad_down[None]


def solution(mesh):
    token = P("expert", "head")
    weight = P("expert", None, "head")
    return jax.shard_map(
        shards,
        mesh=mesh,
        in_specs=(token, P("head", "expert"), token, P("head"), P("head", None), P("expert", None), token)
        + (weight,) * 3,
        out_specs=(token,) + (weight,) * 3,
        check_vma=False,
    )
```

```python
import functools

import jax
import jax.numpy as jnp
from jax import lax
from jax.experimental import pallas as pl
from jax.experimental.pallas import tpu as pltpu
from jax.sharding import PartitionSpec as P

EPSILON = 1e-05
MESH = pl.DeviceIdType.MESH
BF = jnp.bfloat16
F32 = jnp.float32
MIB = 2**20


def coords():
    e, h = lax.axis_index("expert"), lax.axis_index("head")
    return e % 4, h // 2, e // 4, h % 2


def dev(x, y, z, c):
    return {"expert": z * 4 + x, "head": 2 * y + c}


def rot(i, k):
    return lax.rem(i + (k + 4), 4)


def contract(a, b, ca, cb, **kw):
    return lax.dot_general(
        a, b, (((ca,), (cb,)), ((), ())), preferred_element_type=F32, **kw
    )


class Net:
    def __init__(self, ssem, rsem, mate):
        self.ssem, self.rsem, self.mate = ssem, rsem, mate
        self.n, self.sent = 0, []

    def send(self, src, dst, to):
        tag = self.n
        self.n += 1
        copy = pltpu.make_async_remote_copy(
            src_ref=src,
            dst_ref=dst,
            send_sem=self.ssem.at[tag],
            recv_sem=self.rsem.at[tag],
            device_id=to,
            device_id_type=MESH,
        )
        copy.start()
        self.sent.append(copy)
        return tag

    def wait(self, tag, dst):
        pltpu.make_async_remote_copy(
            src_ref=dst,
            dst_ref=dst,
            send_sem=self.ssem.at[tag],
            recv_sem=self.rsem.at[tag],
            device_id=self.mate,
            device_id_type=MESH,
        ).wait_recv()

    def drain(self):
        for copy in self.sent:
            copy.wait_send()
        self.sent = []


class Gather:
    def __init__(self, net, at, a, b, to_a, to_b, lo, hi, share):
        self.net, self.at, self.a, self.b = net, at, a, b
        self.to_a, self.to_b, self.lo, self.hi, self.share = to_a, to_b, lo, hi, share
        self.t = {}

    def ref(self, ka, kb):
        return self.at(rot(self.a, ka), rot(self.b, kb))

    def along_b(self, ka):
        r = self.ref(ka, 0)
        self.t[ka, -1] = self.net.send(r, r, self.to_b(1))
        self.t[ka, 1] = self.net.send(r, r, self.to_b(-1))

    def begin(self):
        r = self.ref(0, 0)
        self.t["a", -1] = self.net.send(r, r, self.to_a(1))
        self.t["a", 1] = self.net.send(r, r, self.to_a(-1))
        self.along_b(0)
        self.share(0, 0)

    def near_a(self):
        for k, part in ((-1, self.lo), (1, self.hi)):
            r = self.ref(k, 0)
            self.net.wait(self.t["a", k], r)
            self.t["f", k] = self.net.send(r.at[part], r.at[part], self.to_a(-k))
            self.along_b(k)
            self.share(k, 0)

    def far_a(self):
        r = self.ref(2, 0)
        self.net.wait(self.t["f", -1], r.at[self.lo])
        self.net.wait(self.t["f", 1], r.at[self.hi])
        self.along_b(2)
        self.share(2, 0)

    def near_b(self, ka):
        for k, part in ((-1, self.lo), (1, self.hi)):
            r = self.ref(ka, k)
            self.net.wait(self.t[ka, k], r)
            self.t["f", ka, k] = self.net.send(r.at[part], r.at[part], self.to_b(-k))
            self.share(ka, k)

    def far_b(self, ka):
        r = self.ref(ka, 2)
        self.net.wait(self.t["f", ka, -1], r.at[self.lo])
        self.net.wait(self.t["f", ka, 1], r.at[self.hi])
        self.share(ka, 2)


def greet(devices, extra=()):
    barrier = pltpu.get_barrier_semaphore()
    for d in devices:
        pl.semaphore_signal(barrier, inc=1, device_id=d, device_id_type=MESH)
    count = len(devices)
    for d, mine in extra:

        @pl.when(jnp.logical_not(mine))
        def _(d=d):
            pl.semaphore_signal(barrier, inc=1, device_id=d, device_id_type=MESH)

        count = count + jnp.where(mine, 0, 1)
    pl.semaphore_wait(barrier, count)


def slot_masks(rts_ref, capacity):
    r0, r1 = rts_ref[0:1, :], rts_ref[1:2, :]
    n = r0.shape[1]
    ids = lax.broadcasted_iota(jnp.int32, (8, n), 0)
    hits = ((r0 == ids) | (r1 == ids)).astype(F32).astype(BF)
    before = (
        lax.broadcasted_iota(jnp.int32, (n, n), 0)
        < lax.broadcasted_iota(jnp.int32, (n, n), 1)
    ).astype(F32).astype(BF)
    earlier = contract(hits, before, 1, 0)
    slot0 = jnp.sum(jnp.where(r0 == ids, earlier, 0.0), axis=0, keepdims=True)
    slot1 = jnp.sum(jnp.where(r1 == ids, earlier, 0.0), axis=0, keepdims=True)
    rows = lax.broadcasted_iota(jnp.int32, (capacity, n), 0)
    slot0, slot1 = slot0.astype(jnp.int32), slot1.astype(jnp.int32)
    return [
        ((r0 == e) & (slot0 == rows), (r1 == e) & (slot1 == rows)) for e in range(4)
    ]


def as_column(row):
    n = row.shape[1]
    eye = lax.broadcasted_iota(jnp.int32, (n, n), 0) == lax.broadcasted_iota(
        jnp.int32, (n, n), 1
    )
    return jnp.sum(jnp.where(eye, row, 0.0), axis=1, keepdims=True)


def layer_kernel(
    att, op, res, gain, rt, rts, cot, gate_h, up_h, down_h,
    out_h, gg_h, gu_h, gd_h,
    state_o, pr_o,
    attb, own, sib16, sibr, r1, fin, st2, tot16, projr, stat, xrow, crow, xr, cr,
    xb, wcat, wd, cb, acc, hid, sibd, sibdr, dst, dr1, dfin, dhf, dab, yst, yr1, yfin, zs, zr,
    ssem, rsem, lsem,
):
    x, y, z, c = coords()
    h = lax.axis_index("head")
    mate = dev(x, y, z, 1 - c)
    net = Net(ssem, rsem, mate)
    turn = [(dev(2 * c + j, z, y, x // 2), (x == 2 * c + j) & (y == z) & (c == x // 2)) for j in range(2)]
    group = [
        {"expert": lax.axis_index("expert"), "head": lax.rem(h + k, 8)}
        for k in range(1, 8)
    ]
    greet(
        [dev(rot(x, 1), y, z, c), dev(rot(x, -1), y, z, c)]
        + [dev(x, y, rot(z, k), c) for k in (1, 2, 3)]
        + group,
        turn,
    )
    weights = [
        pltpu.make_async_copy(gate_h, wcat.at[:, :, pl.ds(0, 256)], lsem.at[1]),
        pltpu.make_async_copy(up_h, wcat.at[:, :, pl.ds(256, 256)], lsem.at[2]),
        pltpu.make_async_copy(down_h, wd, lsem.at[3]),
    ]
    for copy in weights:
        copy.start()
    attb[z, x] = att[...].reshape(attb.shape[2:])

    def quiet(ka, kb):
        pass

    lo, hi = pl.ds(0, 32), pl.ds(32, 32)
    g0 = Gather(net, lambda a, b: attb.at[b, a, 0], x, z, lambda k: dev(rot(x, k), y, z, c), lambda k: dev(x, y, rot(z, k), c), lo, hi, quiet)
    g1 = Gather(net, lambda a, b: attb.at[a, b, 1], z, x, lambda k: dev(x, y, rot(z, k), c), lambda k: dev(rot(x, k), y, z, c), lo, hi, quiet)
    flows = (g0, g1)
    for g in flows:
        g.begin()
    capacity = xrow.shape[1]
    masks = slot_masks(rts, capacity)
    for e, (m0, m1) in enumerate(masks):
        pick = (m0 | m1).astype(F32).astype(BF)
        crow[e] = contract(pick, cot[...], 1, 0).astype(BF)
    for g in flows:
        g.near_a()
    for g in flows:
        g.near_b(0)
    for g in flows:
        g.far_a()
    for k in (-1, 1):
        for g in flows:
            g.near_b(k)
    for k in (0, -1):
        for g in flows:
            g.far_b(k)
    for g in flows:
        g.near_b(2)
    for k in (1, 2):
        for g in flows:
            g.far_b(k)

    def product(yy, cc):
        rows = attb[yy, pl.ds(2 * cc, 2)].reshape(256, att.shape[1])
        return contract(rows, op[...], 1, 0)

    tags = {}
    for k in (2, -1, 1, 0):
        yy = rot(y, k)
        sib16[yy] = product(yy, 1 - c).astype(BF)
        tags[k] = net.send(sib16.at[yy], sibr.at[yy], mate)
    for k in (2, -1, 1, 0):
        yy = rot(y, k)
        own[yy] = product(yy, c)
    for k in (2, -1, 1, 0):
        yy = rot(y, k)
        net.wait(tags[k], sibr.at[yy])
        own[yy] += sibr[yy].astype(F32)
        if k == 2:
            st2[0] = own[yy].astype(BF)
            ta = net.send(st2.at[0, pl.ds(0, 128)], r1.at[0], dev(x, rot(y, 1), z, c))
            tb = net.send(
                st2.at[0, pl.ds(128, 128)], r1.at[1], dev(x, rot(y, -1), z, c)
            )
    net.wait(ta, r1.at[0])
    yy = rot(y, 1)
    own[yy, 0:128, :] += r1[0].astype(F32)
    st2[1] = own[yy].astype(BF)
    tc = net.send(st2.at[1], fin.at[0], dev(x, yy, z, c))
    net.wait(tb, r1.at[1])
    yy = rot(y, -1)
    own[yy, 128:256, :] += r1[1].astype(F32)
    st2[2] = own[yy].astype(BF)
    td = net.send(st2.at[2], fin.at[1], dev(x, yy, z, c))
    net.wait(tc, fin.at[0])
    net.wait(td, fin.at[1])
    total = own[y] + fin[0].astype(F32) + fin[1].astype(F32)
    tot16[...] = total.reshape(tot16.shape).astype(BF)

    base = net.n
    net.n += 2
    i = x % 2
    for j, (d, mine) in enumerate(turn):

        def remote(j=j, d=d):
            return pltpu.make_async_remote_copy(
                src_ref=tot16.at[j],
                dst_ref=projr.at[i],
                send_sem=ssem.at[base + j],
                recv_sem=rsem.at[base + i],
                device_id=d,
                device_id_type=MESH,
            )

        @pl.when(mine)
        def _(j=j):
            pltpu.make_async_copy(tot16.at[j], projr.at[i], lsem.at[0]).start()

        @pl.when(jnp.logical_not(mine))
        def _(remote=remote):
            remote().start()

    for k in range(2):
        local = (x == 2 * c + k) & (y == z) & (c == x // 2)

        @pl.when(local)
        def _(k=k):
            pltpu.make_async_copy(tot16.at[0], projr.at[k], lsem.at[0]).wait()

        @pl.when(jnp.logical_not(local))
        def _(k=k):
            net.wait(base + k, projr.at[k])

    for j, (d, mine) in enumerate(turn):

        @pl.when(jnp.logical_not(mine))
        def _(j=j, d=d):
            pltpu.make_async_remote_copy(
                src_ref=tot16.at[j],
                dst_ref=projr.at[i],
                send_sem=ssem.at[base + j],
                recv_sem=rsem.at[base + i],
                device_id=d,
                device_id_type=MESH,
            ).wait_send()

    half = projr.shape[2]
    for k in range(2):
        cols = slice(k * half, (k + 1) * half)
        state_o[:, cols] = res[:, cols].astype(F32) + projr[k].astype(F32)
    state = state_o[...]
    scaled = state * gain[...].astype(F32)
    stat[h, 0:4, :] = contract(rt[...], scaled, 1, 1, precision=lax.Precision.HIGHEST)
    ones = jnp.ones((8, state.shape[1]), F32)
    squares = contract(ones, state * state, 1, 1, precision=lax.Precision.HIGHEST)
    stat[h, 4:8, :] = squares[0:4]
    tags = [net.send(stat.at[h], stat.at[h], d) for d in group]
    for k, tag in enumerate(tags):
        net.wait(tag, stat.at[lax.rem(h + 7 - k, 8)])
    sums = stat[0]
    for k in range(1, 8):
        sums = sums + stat[k]
    width = 8.0 * state.shape[1]
    inverse = lax.rsqrt(sums[4:5] / width + EPSILON)
    logits = sums[0:4] * inverse
    ids = lax.broadcasted_iota(jnp.int32, logits.shape, 0)
    l0 = jnp.sum(jnp.where(rts[0:1, :] == ids, logits, 0.0), axis=0, keepdims=True)
    l1 = jnp.sum(jnp.where(rts[1:2, :] == ids, logits, 0.0), axis=0, keepdims=True)
    p0, p1 = jax.nn.sigmoid(l0 - l1), jax.nn.sigmoid(l1 - l0)
    pr_o[0:1, :] = p0
    pr_o[1:2, :] = p1
    normed = (scaled * as_column(inverse)).astype(BF)
    for e, (m0, m1) in enumerate(masks):
        pick = (m0 | m1).astype(F32).astype(BF)
        xrow[e] = contract(pick, normed, 1, 0).astype(BF)
    moved = []
    for k in (1, 2, 3):
        e = rot(z, k)
        tag = net.send(xrow.at[e], xr.at[z], dev(x, y, e, c))
        moved.append((tag, xr.at[rot(z, -k)]))
    for e, (m0, m1) in enumerate(masks):
        share = jnp.sum(
            jnp.where(m0, p0, 0.0) + jnp.where(m1, p1, 0.0), axis=1, keepdims=True
        )
        crow[e] = (crow[e].astype(F32) * share).astype(BF)
    xr[z] = xrow[z]
    cr[z] = crow[z]
    for tag, ref in moved:
        net.wait(tag, ref)

    def pair(ref, f):
        return jnp.concatenate(
            [ref[2 * f].astype(F32), ref[2 * f + 1].astype(F32)], axis=0
        ).astype(BF)

    def along_x(k):
        return dev(rot(x, k), y, z, c)

    def along_y(k):
        return dev(x, rot(y, k), z, c)

    def sharing(at):
        tags = {}

        def share(ka, kb, at=at, tags=tags):
            r = at(ka, kb, c)
            tags[ka, kb] = net.send(r, r, mate)

        def arrived(ka, kb, at=at, tags=tags):
            net.wait(tags[ka, kb], at(ka, kb, 1 - c))

        return share, arrived

    for f in range(2):
        xb[y, c, f, x] = pair(xr, f)
    lo, hi = pl.ds(0, 80), pl.ds(80, 64)
    share0, mate0 = sharing(lambda ka, kb, cc: xb.at[rot(y, kb), cc, 0, rot(x, ka)])
    share1, mate1 = sharing(lambda ka, kb, cc: xb.at[rot(y, ka), cc, 1, rot(x, kb)])
    g0 = Gather(net, lambda a, b: xb.at[b, c, 0, a], x, y, along_x, along_y, lo, hi, share0)
    g1 = Gather(net, lambda a, b: xb.at[a, c, 1, b], y, x, along_y, along_x, lo, hi, share1)
    flows = (g0, g1)
    for g in flows:
        g.begin()
    moved = []
    for k in (1, 2, 3):
        e = rot(z, k)
        tag = net.send(crow.at[e], cr.at[z], dev(x, y, e, c))
        moved.append((tag, cr.at[rot(z, -k)]))
    for g in flows:
        g.near_a()
    for g in flows:
        g.near_b(0)
    for g in flows:
        g.far_a()
    for tag, ref in moved:
        net.wait(tag, ref)
    for f in range(2):
        cb[f, x] = pair(cr, f)
    gc = Gather(net, lambda a, b: cb.at[:, b], x, x, along_x, along_x, pl.ds(0, 1), pl.ds(1, 1), quiet)
    for copy in weights:
        copy.wait()

    rows, hidden = xb.shape[4], hid.shape[-1]

    def group0(kb, first):
        for ka in (0, -1, 1, 2):
            mate0(ka, kb)
        yy = rot(y, kb)
        for cc in range(2):
            part = contract(
                xb[yy, cc, 0].reshape(4 * rows, xb.shape[5]), wcat[2 * yy + cc], 1, 0
            ).reshape(4, rows, 2 * hidden)
            if first and cc == 0:
                acc[0] = part
            else:
                acc[0] += part

    def group1(kb):
        for ka in (0, -1, 1, 2):
            mate1(ka, kb)
        xx = rot(x, kb)
        total = jnp.zeros((rows, 2 * hidden), F32)
        for h2 in range(8):
            total += contract(xb[h2 // 2, h2 % 2, 1, xx], wcat[h2], 1, 0)
        acc[1, xx] = total

    for g in flows:
        g.near_b(-1)
    group0(0, True)
    for g in flows:
        g.near_b(1)
    group1(0)
    gc.along_b(0)
    for k in (0, -1):
        for g in flows:
            g.far_b(k)
    for g in flows:
        g.near_b(2)
    group1(-1)
    group1(1)
    group0(-1, False)
    group0(1, False)
    for k in (1, 2):
        for g in flows:
            g.far_b(k)
    gc.near_b(0)

    hshare, hmate = [], []
    hg = []
    for f in range(2):
        s, m = sharing(lambda ka, kb, cc, f=f: hid.at[rot(y, kb), cc, f])
        hmate.append(m)
        hg.append(Gather(net, lambda a, b, f=f: hid.at[b, c, f], y, y, along_y, along_y, pl.ds(0, 2), pl.ds(2, 2), s))
        hshare.append(s)

    def activate(f):
        a, b = acc[f, :, :, 0:hidden], acc[f, :, :, hidden : 2 * hidden]
        hid[y, c, f] = (jax.nn.silu(a) * b).astype(BF)
        hg[f].along_b(0)
        hshare[f](0, 0)

    group1(2)
    activate(1)
    group0(2, False)
    activate(0)
    gc.far_b(0)

    def grad_hidden(yy, cc):
        c_rows = cb[...].reshape(8 * rows, cb.shape[3])
        return contract(c_rows, wd[2 * yy + cc], 1, 1).reshape(2, 4, rows, hidden)

    tags = {}
    for k in (2, -1, 1, 0):
        yy = rot(y, k)
        sibd[yy] = grad_hidden(yy, 1 - c).astype(BF)
        tags[k] = net.send(sibd.at[yy], sibdr.at[yy], mate)
    for f in (1, 0):
        hg[f].near_b(0)
    yy = rot(y, 2)
    net.wait(tags[2], sibdr.at[yy])
    dst[0] = (grad_hidden(yy, c) + sibdr[yy].astype(F32)).astype(BF)
    ta = net.send(dst.at[0, 0], dr1.at[0], along_y(1))
    tb = net.send(dst.at[0, 1], dr1.at[1], along_y(-1))
    for f in (1, 0):
        hg[f].far_b(0)
    for f in (1, 0):
        for kb in (0, -1, 1, 2):
            hmate[f](0, kb)

    def product_y(xx):
        total = jnp.zeros((2 * rows, wd.shape[2]), F32)
        for h2 in range(8):
            part = hid[h2 // 2, h2 % 2, :, xx].reshape(2 * rows, hidden)
            total += contract(part, wd[h2], 1, 0)
        return total.reshape(2, rows, wd.shape[2])

    yst[0] = product_y(rot(x, 2)).astype(BF)
    tya = net.send(yst.at[0, 0], yr1.at[0], along_x(1))
    tyb = net.send(yst.at[0, 1], yr1.at[1], along_x(-1))
    for k, t, i in ((1, ta, 0), (-1, tb, 1)):
        yy = rot(y, k)
        net.wait(tags[k], sibdr.at[yy])
        dhf[...] = grad_hidden(yy, c) + sibdr[yy].astype(F32)
        net.wait(t, dr1.at[i])
        dhf[i] += dr1[i].astype(F32)
        dst[1 + i] = dhf[...].astype(BF)
        tags["f", k] = net.send(dst.at[1 + i], dfin.at[i], along_y(k))
    for k, t, i in ((1, tya, 0), (-1, tyb, 1)):
        total = product_y(rot(x, k))
        net.wait(t, yr1.at[i])
        yst[1 + i, i] = (total[i] + yr1[i].astype(F32)).astype(BF)
        yst[1 + i, 1 - i] = total[1 - i].astype(BF)
        tags["y", k] = net.send(yst.at[1 + i], yfin.at[i], along_x(k))
    total = product_y(x)
    net.wait(tags[0], sibdr.at[y])
    dhf[...] = grad_hidden(y, c) + sibdr[y].astype(F32)
    net.wait(tags["y", 1], yfin.at[0])
    net.wait(tags["y", -1], yfin.at[1])
    total += yfin[0].astype(F32) + yfin[1].astype(F32)
    for zz in range(4):
        zs[zz] = total[zz // 2, (zz % 2) * zs.shape[1] : (zz % 2 + 1) * zs.shape[1]].astype(BF)
    moved = []
    for k in (1, 2, 3):
        e = rot(z, k)
        tag = net.send(zs.at[e], zr.at[z], dev(x, y, e, c))
        moved.append((tag, zr.at[rot(z, -k)]))
    zr[z] = zs[z]

    writes = []

    def write(src, dst_ref, sem):
        copy = pltpu.make_async_copy(src, dst_ref, sem)
        copy.start()
        writes.append(copy)

    for h2 in range(8):
        part = hid[h2 // 2, h2 % 2].reshape(8 * rows, hidden)
        wd[h2] = contract(part, cb[...].reshape(8 * rows, cb.shape[3]), 0, 0).astype(BF)
        write(wd.at[h2], gd_h.at[h2], lsem.at[4 + h2])
    for i, k in ((0, 1), (1, -1)):
        net.wait(tags["f", k], dfin.at[i])
    for f in range(2):
        dh = dhf[f] + dfin[0, f].astype(F32) + dfin[1, f].astype(F32)
        a, b = acc[f, :, :, 0:hidden], acc[f, :, :, hidden : 2 * hidden]
        s = jax.nn.sigmoid(a)
        dab[f, :, :, 0:hidden] = (dh * b * s * (1.0 + a * (1.0 - s))).astype(BF)
        dab[f, :, :, hidden : 2 * hidden] = (dh * (a * s)).astype(BF)
    for h2 in range(8):
        part = xb[h2 // 2, h2 % 2].reshape(8 * rows, xb.shape[5])
        wcat[h2] = contract(
            part, dab[...].reshape(8 * rows, 2 * hidden), 0, 0
        ).astype(BF)
        write(wcat.at[h2, :, pl.ds(0, hidden)], gg_h.at[h2], lsem.at[12 + h2])
        write(wcat.at[h2, :, pl.ds(hidden, hidden)], gu_h.at[h2], lsem.at[20 + h2])

    for tag, ref in moved:
        net.wait(tag, ref)
    took0 = jnp.zeros(state_o.shape, F32)
    took1 = jnp.zeros(state_o.shape, F32)
    for e, (m0, m1) in enumerate(slot_masks(rts, capacity)):
        took0 += contract(m0.astype(F32).astype(BF), zr[e], 0, 0)
        took1 += contract(m1.astype(F32).astype(BF), zr[e], 0, 0)
    out_h[...] = (
        state_o[...] + as_column(pr_o[0:1, :]) * took0 + as_column(pr_o[1:2, :]) * took1
    )
    for copy in writes:
        copy.wait()
    net.drain()


def shards(
    attention, out_proj, residual, norm_gain, router, routes, cotangent,
    gate_weight, up_weight, down_weight,
):
    vmem = pl.BlockSpec(memory_space=pltpu.VMEM)
    hbm = pl.BlockSpec(memory_space=pl.ANY)
    rows, cols = attention.shape
    width = out_proj.shape[1]
    cap = rows * 9 // 16
    pair_rows = 2 * cap
    hidden = gate_weight.shape[2]
    sds = jax.ShapeDtypeStruct
    layer_out, grad_gate, grad_up, grad_down = pl.pallas_call(
        layer_kernel,
        out_shape=(
            sds((rows, cols), F32),
            sds((8, cols, hidden), BF),
            sds((8, cols, hidden), BF),
            sds((8, hidden, cols), BF),
        ),
        in_specs=[vmem] * 7 + [hbm] * 3,
        out_specs=(vmem,) + (hbm,) * 3,
        scratch_shapes=[
            pltpu.VMEM((rows, cols), F32),
            pltpu.VMEM((8, rows), F32),
            pltpu.VMEM((4, 4, 2, rows // 2, cols), BF),
            pltpu.VMEM((4, 2 * rows, width), F32),
            pltpu.VMEM((4, 2 * rows, width), BF),
            pltpu.VMEM((4, 2 * rows, width), BF),
            pltpu.VMEM((2, rows, width), BF),
            pltpu.VMEM((2, 2 * rows, width), BF),
            pltpu.VMEM((3, 2 * rows, width), BF),
            pltpu.VMEM((2, rows, width), BF),
            pltpu.VMEM((2, rows, width), BF),
            pltpu.VMEM((8, 8, rows), F32),
            pltpu.VMEM((4, cap, cols), BF),
            pltpu.VMEM((4, cap, cols), BF),
            pltpu.VMEM((4, cap, cols), BF),
            pltpu.VMEM((4, cap, cols), BF),
            pltpu.VMEM((4, 2, 2, 4, pair_rows, cols), BF),
            pltpu.VMEM((8, cols, 2 * hidden), BF),
            pltpu.VMEM((8, hidden, cols), BF),
            pltpu.VMEM((2, 4, pair_rows, cols), BF),
            pltpu.VMEM((2, 4, pair_rows, 2 * hidden), F32),
            pltpu.VMEM((4, 2, 2, 4, pair_rows, hidden), BF),
            pltpu.VMEM((4, 2, 4, pair_rows, hidden), BF),
            pltpu.VMEM((4, 2, 4, pair_rows, hidden), BF),
            pltpu.VMEM((3, 2, 4, pair_rows, hidden), BF),
            pltpu.VMEM((2, 4, pair_rows, hidden), BF),
            pltpu.VMEM((2, 2, 4, pair_rows, hidden), BF),
            pltpu.VMEM((2, 4, pair_rows, hidden), F32),
            pltpu.VMEM((2, 4, pair_rows, 2 * hidden), BF),
            pltpu.VMEM((3, 2, pair_rows, cols), BF),
            pltpu.VMEM((2, pair_rows, cols), BF),
            pltpu.VMEM((2, 2, pair_rows, cols), BF),
            pltpu.VMEM((4, cap, cols), BF),
            pltpu.VMEM((4, cap, cols), BF),
            pltpu.SemaphoreType.DMA((208,)),
            pltpu.SemaphoreType.DMA((208,)),
            pltpu.SemaphoreType.DMA((28,)),
        ],
        compiler_params=pltpu.CompilerParams(
            collective_id=0, has_side_effects=True, vmem_limit_bytes=63 * MIB
        ),
        cost_estimate=pl.CostEstimate(
            flops=30_000_000_000, bytes_accessed=25_000_000, transcendentals=0
        ),
    )(
        attention,
        out_proj,
        residual,
        norm_gain[None, :],
        router.T,
        routes.T,
        cotangent,
        gate_weight.reshape(8, cols, hidden),
        up_weight.reshape(8, cols, hidden),
        down_weight.reshape(8, hidden, cols),
    )
    return (
        layer_out,
        grad_gate.reshape(gate_weight.shape),
        grad_up.reshape(up_weight.shape),
        grad_down.reshape(down_weight.shape),
    )


def solution(mesh):
    token = P("expert", "head")
    weight = P("expert", None, "head")
    return jax.shard_map(
        shards,
        mesh=mesh,
        in_specs=(token, P("head", "expert"), token, P("head"), P("head", None), P("expert", None), token)
        + (weight,) * 3,
        out_specs=(token,) + (weight,) * 3,
        check_vma=False,
    )
```

```python
import functools

import jax
import jax.numpy as jnp
from jax import lax
from jax.experimental import pallas as pl
from jax.experimental.pallas import tpu as pltpu
from jax.sharding import PartitionSpec as P

EPSILON = 1e-05
MESH = pl.DeviceIdType.MESH
BF = jnp.bfloat16
F32 = jnp.float32
MIB = 2**20


def coords():
    e, h = lax.axis_index("expert"), lax.axis_index("head")
    return e % 4, h // 2, e // 4, h % 2


def dev(x, y, z, c):
    return {"expert": z * 4 + x, "head": 2 * y + c}


def rot(i, k):
    return lax.rem(i + (k + 4), 4)


def contract(a, b, ca, cb, **kw):
    return lax.dot_general(
        a, b, (((ca,), (cb,)), ((), ())), preferred_element_type=F32, **kw
    )


class Net:
    def __init__(self, ssem, rsem, mate):
        self.ssem, self.rsem, self.mate = ssem, rsem, mate
        self.n, self.sent = 0, {}

    def send(self, src, dst, to):
        tag = self.n
        self.n += 1
        copy = pltpu.make_async_remote_copy(
            src_ref=src,
            dst_ref=dst,
            send_sem=self.ssem.at[tag],
            recv_sem=self.rsem.at[tag],
            device_id=to,
            device_id_type=MESH,
        )
        copy.start()
        self.sent[tag] = copy
        return tag

    def wait(self, tag, dst):
        pltpu.make_async_remote_copy(
            src_ref=dst,
            dst_ref=dst,
            send_sem=self.ssem.at[tag],
            recv_sem=self.rsem.at[tag],
            device_id=self.mate,
            device_id_type=MESH,
        ).wait_recv()

    def drain(self):
        for tag in list(self.sent):
            self.left(tag)

    def left(self, tag):
        self.sent.pop(tag).wait_send()


class Gather:
    def __init__(self, net, at, a, b, to_a, to_b, lo, hi, share):
        self.net, self.at, self.a, self.b = net, at, a, b
        self.to_a, self.to_b, self.lo, self.hi, self.share = to_a, to_b, lo, hi, share
        self.t = {}

    def ref(self, ka, kb):
        return self.at(rot(self.a, ka), rot(self.b, kb))

    def along_b(self, ka):
        r = self.ref(ka, 0)
        self.t[ka, -1] = self.net.send(r, r, self.to_b(1))
        self.t[ka, 1] = self.net.send(r, r, self.to_b(-1))

    def begin(self):
        r = self.ref(0, 0)
        self.t["a", -1] = self.net.send(r, r, self.to_a(1))
        self.t["a", 1] = self.net.send(r, r, self.to_a(-1))
        self.along_b(0)
        self.share(0, 0)

    def near_a(self):
        for k, part in ((-1, self.lo), (1, self.hi)):
            r = self.ref(k, 0)
            self.net.wait(self.t["a", k], r)
            self.t["f", k] = self.net.send(r.at[part], r.at[part], self.to_a(-k))
            self.along_b(k)
            self.share(k, 0)

    def far_a(self):
        r = self.ref(2, 0)
        self.net.wait(self.t["f", -1], r.at[self.lo])
        self.net.wait(self.t["f", 1], r.at[self.hi])
        self.along_b(2)
        self.share(2, 0)

    def near_b(self, ka):
        for k, part in ((-1, self.lo), (1, self.hi)):
            r = self.ref(ka, k)
            self.net.wait(self.t[ka, k], r)
            self.t["f", ka, k] = self.net.send(r.at[part], r.at[part], self.to_b(-k))
            self.share(ka, k)

    def far_b(self, ka):
        r = self.ref(ka, 2)
        self.net.wait(self.t["f", ka, -1], r.at[self.lo])
        self.net.wait(self.t["f", ka, 1], r.at[self.hi])
        self.share(ka, 2)


def greet(devices, extra=()):
    barrier = pltpu.get_barrier_semaphore()
    for d in devices:
        pl.semaphore_signal(barrier, inc=1, device_id=d, device_id_type=MESH)
    count = len(devices)
    for d, mine in extra:

        @pl.when(jnp.logical_not(mine))
        def _(d=d):
            pl.semaphore_signal(barrier, inc=1, device_id=d, device_id_type=MESH)

        count = count + jnp.where(mine, 0, 1)
    pl.semaphore_wait(barrier, count)


def slot_masks(rts_ref, capacity):
    r0, r1 = rts_ref[0:1, :], rts_ref[1:2, :]
    n = r0.shape[1]
    ids = lax.broadcasted_iota(jnp.int32, (8, n), 0)
    hits = ((r0 == ids) | (r1 == ids)).astype(F32).astype(BF)
    before = (
        lax.broadcasted_iota(jnp.int32, (n, n), 0)
        < lax.broadcasted_iota(jnp.int32, (n, n), 1)
    ).astype(F32).astype(BF)
    earlier = contract(hits, before, 1, 0)
    slot0 = jnp.sum(jnp.where(r0 == ids, earlier, 0.0), axis=0, keepdims=True)
    slot1 = jnp.sum(jnp.where(r1 == ids, earlier, 0.0), axis=0, keepdims=True)
    rows = lax.broadcasted_iota(jnp.int32, (capacity, n), 0)
    slot0, slot1 = slot0.astype(jnp.int32), slot1.astype(jnp.int32)
    return [
        ((r0 == e) & (slot0 == rows), (r1 == e) & (slot1 == rows)) for e in range(4)
    ]


def as_column(row):
    n = row.shape[1]
    eye = lax.broadcasted_iota(jnp.int32, (n, n), 0) == lax.broadcasted_iota(
        jnp.int32, (n, n), 1
    )
    return jnp.sum(jnp.where(eye, row, 0.0), axis=1, keepdims=True)


def layer_kernel(
    att, op, res, gain, rt, rts, cot, gate_h, up_h, down_h,
    out_h, gg_h, gu_h, gd_h,
    state_o, pr_o,
    attb, own, sib16, sibr, r1, fin, st2, tot16, projr, stat, xrow, crow, xr, cr,
    xb, wcat, wd, cb, acc, hid, sibd, sibdr, dst, dr1, dfin, dhf, dab, pcol, prow, pz, pall, yst, yr1, yfin, ysum, yvia, zs, zr,
    ssem, rsem, lsem,
):
    x, y, z, c = coords()
    h = lax.axis_index("head")
    mate = dev(x, y, z, 1 - c)
    net = Net(ssem, rsem, mate)
    turn = [(dev(2 * c + j, z, y, x // 2), (x == 2 * c + j) & (y == z) & (c == x // 2)) for j in range(2)]
    group = [
        {"expert": lax.axis_index("expert"), "head": lax.rem(h + k, 8)}
        for k in range(1, 8)
    ]
    greet(
        [dev(rot(x, k), y, z, c) for k in (1, 2, 3)]
        + [dev(x, y, rot(z, k), c) for k in (1, 2, 3)]
        + group,
        turn,
    )
    weights = [
        pltpu.make_async_copy(gate_h, wcat.at[:, :, pl.ds(0, 256)], lsem.at[1]),
        pltpu.make_async_copy(up_h, wcat.at[:, :, pl.ds(256, 256)], lsem.at[2]),
        pltpu.make_async_copy(down_h, wd, lsem.at[3]),
    ]
    for copy in weights:
        copy.start()
    attb[z, x] = att[...].reshape(attb.shape[2:])

    def quiet(ka, kb):
        pass

    def pair(ref, f):
        return jnp.concatenate(
            [ref[2 * f].astype(F32), ref[2 * f + 1].astype(F32)], axis=0
        ).astype(BF)

    def along_x(k):
        return dev(rot(x, k), y, z, c)

    def along_y(k):
        return dev(x, rot(y, k), z, c)

    lo, hi = pl.ds(0, 32), pl.ds(32, 32)
    g0 = Gather(net, lambda a, b: attb.at[b, a, 0], x, z, lambda k: dev(rot(x, k), y, z, c), lambda k: dev(x, y, rot(z, k), c), lo, hi, quiet)
    g1 = Gather(net, lambda a, b: attb.at[a, b, 1], z, x, lambda k: dev(x, y, rot(z, k), c), lambda k: dev(rot(x, k), y, z, c), lo, hi, quiet)
    flows = (g0, g1)
    for g in flows:
        g.begin()
    capacity = xrow.shape[1]
    masks = slot_masks(rts, capacity)
    for e, (m0, m1) in enumerate(masks):
        pick = (m0 | m1).astype(F32).astype(BF)
        crow[e] = contract(pick, cot[...], 1, 0).astype(BF)
    cr[z] = crow[z]
    for g in flows:
        g.near_a()
    for g in flows:
        g.near_b(0)
    for g in flows:
        g.far_a()
    for k in (-1, 1):
        for g in flows:
            g.near_b(k)
    for k in (0, -1):
        for g in flows:
            g.far_b(k)
    for g in flows:
        g.near_b(2)
    cmoved = []
    for k in (1, 2, 3):
        e = rot(z, k)
        tag = net.send(crow.at[e], cr.at[z], dev(x, y, e, c))
        cmoved.append((tag, cr.at[rot(z, -k)]))
    for k in (1, 2):
        for g in flows:
            g.far_b(k)

    def product(yy, cc):
        rows = attb[yy, pl.ds(2 * cc, 2)].reshape(256, att.shape[1])
        return contract(rows, op[...], 1, 0)

    tags = {}
    for k in (2, -1, 1, 0):
        yy = rot(y, k)
        sib16[yy] = product(yy, 1 - c).astype(BF)
        tags[k] = net.send(sib16.at[yy], sibr.at[yy], mate)
    for k in (2, -1, 1, 0):
        yy = rot(y, k)
        own[yy] = product(yy, c)
    for k in (2, -1, 1, 0):
        yy = rot(y, k)
        net.wait(tags[k], sibr.at[yy])
        own[yy] += sibr[yy].astype(F32)
        if k == 2:
            st2[0] = own[yy].astype(BF)
            ta = net.send(st2.at[0, pl.ds(0, 128)], r1.at[0], dev(x, rot(y, 1), z, c))
            tb = net.send(
                st2.at[0, pl.ds(128, 128)], r1.at[1], dev(x, rot(y, -1), z, c)
            )
    for tag, ref in cmoved:
        net.wait(tag, ref)
    for f in range(2):
        cb[f, x] = pair(cr, f)
    gc = Gather(net, lambda a, b: cb.at[:, b], x, x, along_x, along_x, pl.ds(0, 1), pl.ds(1, 1), quiet)
    gc.along_b(0)
    net.wait(ta, r1.at[0])
    yy = rot(y, 1)
    own[yy, 0:128, :] += r1[0].astype(F32)
    st2[1] = own[yy].astype(BF)
    tc = net.send(st2.at[1], fin.at[0], dev(x, yy, z, c))
    net.wait(tb, r1.at[1])
    yy = rot(y, -1)
    own[yy, 128:256, :] += r1[1].astype(F32)
    st2[2] = own[yy].astype(BF)
    td = net.send(st2.at[2], fin.at[1], dev(x, yy, z, c))
    net.wait(tc, fin.at[0])
    net.wait(td, fin.at[1])
    total = own[y] + fin[0].astype(F32) + fin[1].astype(F32)
    tot16[...] = total.reshape(tot16.shape).astype(BF)

    base = net.n
    net.n += 2
    i = x % 2
    for j, (d, mine) in enumerate(turn):

        def remote(j=j, d=d):
            return pltpu.make_async_remote_copy(
                src_ref=tot16.at[j],
                dst_ref=projr.at[i],
                send_sem=ssem.at[base + j],
                recv_sem=rsem.at[base + i],
                device_id=d,
                device_id_type=MESH,
            )

        @pl.when(mine)
        def _(j=j):
            pltpu.make_async_copy(tot16.at[j], projr.at[i], lsem.at[0]).start()

        @pl.when(jnp.logical_not(mine))
        def _(remote=remote):
            remote().start()

    gc.near_b(0)
    for k in range(2):
        local = (x == 2 * c + k) & (y == z) & (c == x // 2)

        @pl.when(local)
        def _(k=k):
            pltpu.make_async_copy(tot16.at[0], projr.at[k], lsem.at[0]).wait()

        @pl.when(jnp.logical_not(local))
        def _(k=k):
            net.wait(base + k, projr.at[k])

    for j, (d, mine) in enumerate(turn):

        @pl.when(jnp.logical_not(mine))
        def _(j=j, d=d):
            pltpu.make_async_remote_copy(
                src_ref=tot16.at[j],
                dst_ref=projr.at[i],
                send_sem=ssem.at[base + j],
                recv_sem=rsem.at[base + i],
                device_id=d,
                device_id_type=MESH,
            ).wait_send()

    half = projr.shape[2]
    for k in range(2):
        cols = slice(k * half, (k + 1) * half)
        state_o[:, cols] = res[:, cols].astype(F32) + projr[k].astype(F32)
    state = state_o[...]
    scaled = state * gain[...].astype(F32)
    stat[h, 0:4, :] = contract(rt[...], scaled, 1, 1, precision=lax.Precision.HIGHEST)
    ones = jnp.ones((8, state.shape[1]), F32)
    squares = contract(ones, state * state, 1, 1, precision=lax.Precision.HIGHEST)
    stat[h, 4:8, :] = squares[0:4]
    tags = [net.send(stat.at[h], stat.at[h], d) for d in group]
    rows, hidden = xb.shape[4], hid.shape[-1]
    for copy in weights:
        copy.wait()
    gc.far_b(0)

    def grad_hidden(yy, cc):
        c_rows = cb[...].reshape(8 * rows, cb.shape[3])
        return contract(c_rows, wd[2 * yy + cc], 1, 1).reshape(2, 4, rows, hidden)

    dtags = {}
    for k in (2, -1, 1, 0):
        yy = rot(y, k)
        sibd[yy] = grad_hidden(yy, 1 - c).astype(BF)
        dtags[k] = net.send(sibd.at[yy], sibdr.at[yy], mate)

    for k, tag in enumerate(tags):
        net.wait(tag, stat.at[lax.rem(h + 7 - k, 8)])
    sums = stat[0]
    for k in range(1, 8):
        sums = sums + stat[k]
    width = 8.0 * state.shape[1]
    inverse = lax.rsqrt(sums[4:5] / width + EPSILON)
    logits = sums[0:4] * inverse
    ids = lax.broadcasted_iota(jnp.int32, logits.shape, 0)
    l0 = jnp.sum(jnp.where(rts[0:1, :] == ids, logits, 0.0), axis=0, keepdims=True)
    l1 = jnp.sum(jnp.where(rts[1:2, :] == ids, logits, 0.0), axis=0, keepdims=True)
    p0, p1 = jax.nn.sigmoid(l0 - l1), jax.nn.sigmoid(l1 - l0)
    pr_o[0:1, :] = p0
    pr_o[1:2, :] = p1
    normed = (scaled * as_column(inverse)).astype(BF)
    for e, (m0, m1) in enumerate(masks):
        pick = (m0 | m1).astype(F32).astype(BF)
        xrow[e] = contract(pick, normed, 1, 0).astype(BF)
    moved = []
    for k in (1, 2, 3):
        e = rot(z, k)
        tag = net.send(xrow.at[e], xr.at[z], dev(x, y, e, c))
        moved.append((tag, xr.at[rot(z, -k)]))
    xr[z] = xrow[z]
    both = jnp.concatenate([p0, p1, jnp.zeros((6, p0.shape[1]), F32)], axis=0)
    for e, (m0, m1) in enumerate(masks):
        first = contract(both, m0.astype(F32), 1, 1, precision=lax.Precision.HIGHEST)
        second = contract(both, m1.astype(F32), 1, 1, precision=lax.Precision.HIGHEST)
        prow[e] = jnp.zeros(prow.shape[1:], F32)
        prow[e, 0:1, 0:capacity] = first[0:1] + second[1:2]
    pmoved = []
    for k in (1, 2, 3):
        e = rot(z, k)
        tag = net.send(prow.at[e], pz.at[z], dev(x, y, e, c))
        pmoved.append((tag, pz.at[rot(z, -k)]))
    pz[z] = prow[z]
    yy = rot(y, 2)
    net.wait(dtags[2], sibdr.at[yy])
    dst[0] = (grad_hidden(yy, c) + sibdr[yy].astype(F32)).astype(BF)
    dta = net.send(dst.at[0, 0], dr1.at[0], along_y(1))
    dtb = net.send(dst.at[0, 1], dr1.at[1], along_y(-1))
    for tag, ref in moved:
        net.wait(tag, ref)

    def sharing(at):
        tags = {}

        def share(ka, kb, at=at, tags=tags):
            r = at(ka, kb, c)
            tags[ka, kb] = net.send(r, r, mate)

        def arrived(ka, kb, at=at, tags=tags):
            net.wait(tags[ka, kb], at(ka, kb, 1 - c))

        return share, arrived

    for f in range(2):
        xb[y, c, f, x] = pair(xr, f)
    lo, hi = pl.ds(0, 80), pl.ds(80, 64)
    share0, mate0 = sharing(lambda ka, kb, cc: xb.at[rot(y, kb), cc, 0, rot(x, ka)])
    share1, mate1 = sharing(lambda ka, kb, cc: xb.at[rot(y, ka), cc, 1, rot(x, kb)])
    g0 = Gather(net, lambda a, b: xb.at[b, c, 0, a], x, y, along_x, along_y, lo, hi, share0)
    g1 = Gather(net, lambda a, b: xb.at[a, c, 1, b], y, x, along_y, along_x, lo, hi, share1)
    flows = (g0, g1)
    for g in flows:
        g.begin()
    for g in flows:
        g.near_a()
    for g in flows:
        g.near_b(0)
    for g in flows:
        g.far_a()
    for tag, ref in pmoved:
        net.wait(tag, ref)
    pall[x] = pz[...]
    ptags = []
    for k in (1, 2, 3):
        tag = net.send(pall.at[x], pall.at[x], along_x(k))
        ptags.append((tag, pall.at[rot(x, -k)]))

    def group0(kb, first):
        for ka in (0, -1, 1, 2):
            mate0(ka, kb)
        yy = rot(y, kb)
        for cc in range(2):
            part = contract(
                xb[yy, cc, 0].reshape(4 * rows, xb.shape[5]), wcat[2 * yy + cc], 1, 0
            ).reshape(4, rows, 2 * hidden)
            if first and cc == 0:
                acc[0] = part
            else:
                acc[0] += part

    def group1(kb):
        for ka in (0, -1, 1, 2):
            mate1(ka, kb)
        xx = rot(x, kb)
        total = jnp.zeros((rows, 2 * hidden), F32)
        for h2 in range(8):
            total += contract(xb[h2 // 2, h2 % 2, 1, xx], wcat[h2], 1, 0)
        acc[1, xx] = total

    for g in flows:
        g.near_b(-1)
    group0(0, True)
    for g in flows:
        g.near_b(1)
    group1(0)
    for k in (0, -1):
        for g in flows:
            g.far_b(k)
    for g in flows:
        g.near_b(2)
    for k, t, i in ((1, dta, 0), (-1, dtb, 1)):
        yy = rot(y, k)
        net.wait(dtags[k], sibdr.at[yy])
        dhf[...] = grad_hidden(yy, c) + sibdr[yy].astype(F32)
        net.wait(t, dr1.at[i])
        dhf[i] += dr1[i].astype(F32)
        dst[1 + i] = dhf[...].astype(BF)
        dtags["f", k] = net.send(dst.at[1 + i], dfin.at[i], along_y(k))
    group1(-1)
    group1(1)
    group0(-1, False)
    group0(1, False)
    for k in (1, 2):
        for g in flows:
            g.far_b(k)

    hshare, hmate = [], []
    hg = []
    for f in range(2):
        s, m = sharing(lambda ka, kb, cc, f=f: hid.at[rot(y, kb), cc, f])
        hmate.append(m)
        hg.append(Gather(net, lambda a, b, f=f: hid.at[b, c, f], y, y, along_y, along_y, pl.ds(0, 2), pl.ds(2, 2), s))
        hshare.append(s)

    def activate(f):
        a, b = acc[f, :, :, 0:hidden], acc[f, :, :, hidden : 2 * hidden]
        hid[y, c, f] = (jax.nn.silu(a) * b).astype(BF)
        hg[f].along_b(0)
        hshare[f](0, 0)

    group1(2)
    activate(1)
    group0(2, False)
    activate(0)
    net.wait(dtags[0], sibdr.at[y])
    dhf[...] = grad_hidden(y, c) + sibdr[y].astype(F32)
    for tag, ref in ptags:
        net.wait(tag, ref)
    for tag in gc.t.values():
        net.left(tag)
    for f in range(2):
        for xx in range(4):
            cols = [as_column(pall[xx, 2 * f + i, 0:1, :])[0:capacity] for i in range(2)]
            pcol[f, xx] = jnp.concatenate(cols, axis=0)
            cb[f, xx] = (cb[f, xx].astype(F32) * pcol[f, xx]).astype(BF)

    writes = []

    def write(src, dst_ref, sem):
        copy = pltpu.make_async_copy(src, dst_ref, sem)
        copy.start()
        writes.append(copy)

    def grads(h2):
        part = xb[h2 // 2, h2 % 2].reshape(8 * rows, xb.shape[5])
        wcat[h2] = contract(
            part, dab[...].reshape(8 * rows, 2 * hidden), 0, 0
        ).astype(BF)
        write(wcat.at[h2, :, pl.ds(0, hidden)], gg_h.at[h2], lsem.at[12 + h2])
        write(wcat.at[h2, :, pl.ds(hidden, hidden)], gu_h.at[h2], lsem.at[20 + h2])

    def grads_down(h2):
        part = hid[h2 // 2, h2 % 2].reshape(8 * rows, hidden)
        wd[h2] = contract(part, cb[...].reshape(8 * rows, cb.shape[3]), 0, 0).astype(BF)
        write(wd.at[h2], gd_h.at[h2], lsem.at[4 + h2])

    for i, k in ((0, 1), (1, -1)):
        net.wait(dtags["f", k], dfin.at[i])
    for f in range(2):
        dh = dhf[f] + dfin[0, f].astype(F32) + dfin[1, f].astype(F32)
        dh = dh * pcol[f]
        a, b = acc[f, :, :, 0:hidden], acc[f, :, :, hidden : 2 * hidden]
        s = jax.nn.sigmoid(a)
        dab[f, :, :, 0:hidden] = (dh * b * s * (1.0 + a * (1.0 - s))).astype(BF)
        dab[f, :, :, hidden : 2 * hidden] = (dh * (a * s)).astype(BF)
    def product_y(f, xx):
        total = jnp.zeros((rows, wd.shape[2]), F32)
        for h2 in range(8):
            total += contract(hid[h2 // 2, h2 % 2, f, xx], wd[h2], 1, 0)
        return total

    ytags = {}

    def expert_rows(f, block):
        via = 1 if f == 0 else -1
        yst[0, f] = product_y(f, rot(x, 2)).astype(BF)
        first = net.send(yst.at[0, f], yr1.at[f], along_x(via))
        yst[1, f] = product_y(f, rot(x, -via)).astype(BF)
        ytags[f, -via] = net.send(yst.at[1, f], yfin.at[1, f], along_x(-via))
        yvia[...] = product_y(f, rot(x, via))
        ysum[f] = product_y(f, x)
        grads(block)
        net.wait(first, yr1.at[f])
        yst[2, f] = (yvia[...] + yr1[f].astype(F32)).astype(BF)
        ytags[f, via] = net.send(yst.at[2, f], yfin.at[0, f], along_x(via))

    zbase = net.n
    net.n += 4

    def to_plane(zz):
        return pltpu.make_async_remote_copy(
            src_ref=zs.at[zz],
            dst_ref=zr.at[z],
            send_sem=ssem.at[zbase + zz],
            recv_sem=rsem.at[zbase + z],
            device_id=dev(x, y, zz, c),
            device_id_type=MESH,
        )

    def to_owners(f):
        via = 1 if f == 0 else -1
        net.wait(ytags[f, -via], yfin.at[1, f])
        net.wait(ytags[f, via], yfin.at[0, f])
        total = ysum[f] + yfin[0, f].astype(F32) + yfin[1, f].astype(F32)
        for i in range(2):
            zz = 2 * f + i
            zs[zz] = total[i * capacity : (i + 1) * capacity].astype(BF)

            @pl.when(z != zz)
            def _(zz=zz):
                to_plane(zz).start()

    def arrive(f):
        hg[f].far_b(0)
        for kb in (0, -1, 1, 2):
            hmate[f](0, kb)

    hg[1].near_b(0)
    grads(0)
    hg[0].near_b(0)
    for h2 in (1, 2, 3):
        grads(h2)
    arrive(1)
    expert_rows(1, 4)
    grads(5)
    arrive(0)
    expert_rows(0, 6)
    to_owners(1)
    for h2 in range(6):
        grads_down(h2)
    to_owners(0)
    for h2 in (6, 7):
        grads_down(h2)
    grads(7)
    zr[z] = zs[z]
    for k in (1, 2, 3):
        zz = rot(z, k)
        net.wait(zbase + zz, zr.at[zz])
    for zz in range(4):

        @pl.when(z != zz)
        def _(zz=zz):
            to_plane(zz).wait_send()

    took0 = jnp.zeros(state_o.shape, F32)
    took1 = jnp.zeros(state_o.shape, F32)
    for e, (m0, m1) in enumerate(slot_masks(rts, capacity)):
        took0 += contract(m0.astype(F32).astype(BF), zr[e], 0, 0)
        took1 += contract(m1.astype(F32).astype(BF), zr[e], 0, 0)
    out_h[...] = (
        state_o[...] + as_column(pr_o[0:1, :]) * took0 + as_column(pr_o[1:2, :]) * took1
    )
    for copy in writes:
        copy.wait()
    net.drain()


def shards(
    attention, out_proj, residual, norm_gain, router, routes, cotangent,
    gate_weight, up_weight, down_weight,
):
    vmem = pl.BlockSpec(memory_space=pltpu.VMEM)
    hbm = pl.BlockSpec(memory_space=pl.ANY)
    rows, cols = attention.shape
    width = out_proj.shape[1]
    cap = rows * 9 // 16
    pair_rows = 2 * cap
    hidden = gate_weight.shape[2]
    sds = jax.ShapeDtypeStruct
    layer_out, grad_gate, grad_up, grad_down = pl.pallas_call(
        layer_kernel,
        out_shape=(
            sds((rows, cols), F32),
            sds((8, cols, hidden), BF),
            sds((8, cols, hidden), BF),
            sds((8, hidden, cols), BF),
        ),
        in_specs=[vmem] * 7 + [hbm] * 3,
        out_specs=(vmem,) + (hbm,) * 3,
        scratch_shapes=[
            pltpu.VMEM((rows, cols), F32),
            pltpu.VMEM((8, rows), F32),
            pltpu.VMEM((4, 4, 2, rows // 2, cols), BF),
            pltpu.VMEM((4, 2 * rows, width), F32),
            pltpu.VMEM((4, 2 * rows, width), BF),
            pltpu.VMEM((4, 2 * rows, width), BF),
            pltpu.VMEM((2, rows, width), BF),
            pltpu.VMEM((2, 2 * rows, width), BF),
            pltpu.VMEM((3, 2 * rows, width), BF),
            pltpu.VMEM((2, rows, width), BF),
            pltpu.VMEM((2, rows, width), BF),
            pltpu.VMEM((8, 8, rows), F32),
            pltpu.VMEM((4, cap, cols), BF),
            pltpu.VMEM((4, cap, cols), BF),
            pltpu.VMEM((4, cap, cols), BF),
            pltpu.VMEM((4, cap, cols), BF),
            pltpu.VMEM((4, 2, 2, 4, pair_rows, cols), BF),
            pltpu.VMEM((8, cols, 2 * hidden), BF),
            pltpu.VMEM((8, hidden, cols), BF),
            pltpu.VMEM((2, 4, pair_rows, cols), BF),
            pltpu.VMEM((2, 4, pair_rows, 2 * hidden), F32),
            pltpu.VMEM((4, 2, 2, 4, pair_rows, hidden), BF),
            pltpu.VMEM((4, 2, 4, pair_rows, hidden), BF),
            pltpu.VMEM((4, 2, 4, pair_rows, hidden), BF),
            pltpu.VMEM((3, 2, 4, pair_rows, hidden), BF),
            pltpu.VMEM((2, 4, pair_rows, hidden), BF),
            pltpu.VMEM((2, 2, 4, pair_rows, hidden), BF),
            pltpu.VMEM((2, 4, pair_rows, hidden), F32),
            pltpu.VMEM((2, 4, pair_rows, 2 * hidden), BF),
            pltpu.VMEM((2, 4, pair_rows, 1), F32),
            pltpu.VMEM((4, 8, rows), F32),
            pltpu.VMEM((4, 8, rows), F32),
            pltpu.VMEM((4, 4, 8, rows), F32),
            pltpu.VMEM((3, 2, pair_rows, cols), BF),
            pltpu.VMEM((2, pair_rows, cols), BF),
            pltpu.VMEM((2, 2, pair_rows, cols), BF),
            pltpu.VMEM((2, pair_rows, cols), F32),
            pltpu.VMEM((pair_rows, cols), F32),
            pltpu.VMEM((4, cap, cols), BF),
            pltpu.VMEM((4, cap, cols), BF),
            pltpu.SemaphoreType.DMA((216,)),
            pltpu.SemaphoreType.DMA((216,)),
            pltpu.SemaphoreType.DMA((28,)),
        ],
        compiler_params=pltpu.CompilerParams(
            collective_id=0, has_side_effects=True, vmem_limit_bytes=63 * MIB
        ),
        cost_estimate=pl.CostEstimate(
            flops=30_000_000_000, bytes_accessed=25_000_000, transcendentals=0
        ),
    )(
        attention,
        out_proj,
        residual,
        norm_gain[None, :],
        router.T,
        routes.T,
        cotangent,
        gate_weight.reshape(8, cols, hidden),
        up_weight.reshape(8, cols, hidden),
        down_weight.reshape(8, hidden, cols),
    )
    return (
        layer_out,
        grad_gate.reshape(gate_weight.shape),
        grad_up.reshape(up_weight.shape),
        grad_down.reshape(down_weight.shape),
    )


def solution(mesh):
    token = P("expert", "head")
    weight = P("expert", None, "head")
    return jax.shard_map(
        shards,
        mesh=mesh,
        in_specs=(token, P("head", "expert"), token, P("head"), P("head", None), P("expert", None), token)
        + (weight,) * 3,
        out_specs=(token,) + (weight,) * 3,
        check_vma=False,
    )
```

```python
import functools

import jax
import jax.numpy as jnp
from jax import lax
from jax.experimental import pallas as pl
from jax.experimental.pallas import tpu as pltpu
from jax.sharding import PartitionSpec as P

EPSILON = 1e-05
MESH = pl.DeviceIdType.MESH
BF = jnp.bfloat16
F32 = jnp.float32
MIB = 2**20


def coords():
    e, h = lax.axis_index("expert"), lax.axis_index("head")
    return e % 4, h // 2, e // 4, h % 2


def dev(x, y, z, c):
    return {"expert": z * 4 + x, "head": 2 * y + c}


def rot(i, k):
    return lax.rem(i + (k + 4), 4)


def contract(a, b, ca, cb, **kw):
    return lax.dot_general(
        a, b, (((ca,), (cb,)), ((), ())), preferred_element_type=F32, **kw
    )


class Net:
    def __init__(self, ssem, rsem, mate):
        self.ssem, self.rsem, self.mate = ssem, rsem, mate
        self.n, self.sent = 0, {}

    def send(self, src, dst, to):
        tag = self.n
        self.n += 1
        copy = pltpu.make_async_remote_copy(
            src_ref=src,
            dst_ref=dst,
            send_sem=self.ssem.at[tag],
            recv_sem=self.rsem.at[tag],
            device_id=to,
            device_id_type=MESH,
        )
        copy.start()
        self.sent[tag] = copy
        return tag

    def wait(self, tag, dst):
        pltpu.make_async_remote_copy(
            src_ref=dst,
            dst_ref=dst,
            send_sem=self.ssem.at[tag],
            recv_sem=self.rsem.at[tag],
            device_id=self.mate,
            device_id_type=MESH,
        ).wait_recv()

    def drain(self):
        for tag in list(self.sent):
            self.left(tag)

    def left(self, tag):
        self.sent.pop(tag).wait_send()


class Gather:
    def __init__(self, net, at, a, b, to_a, to_b, lo, hi, share):
        self.net, self.at, self.a, self.b = net, at, a, b
        self.to_a, self.to_b, self.lo, self.hi, self.share = to_a, to_b, lo, hi, share
        self.t = {}

    def ref(self, ka, kb):
        return self.at(rot(self.a, ka), rot(self.b, kb))

    def along_b(self, ka):
        r = self.ref(ka, 0)
        self.t[ka, -1] = self.net.send(r, r, self.to_b(1))
        self.t[ka, 1] = self.net.send(r, r, self.to_b(-1))

    def begin(self):
        r = self.ref(0, 0)
        self.t["a", -1] = self.net.send(r, r, self.to_a(1))
        self.t["a", 1] = self.net.send(r, r, self.to_a(-1))
        self.along_b(0)
        self.share(0, 0)

    def near_a(self):
        for k, part in ((-1, self.lo), (1, self.hi)):
            r = self.ref(k, 0)
            self.net.wait(self.t["a", k], r)
            self.t["f", k] = self.net.send(r.at[part], r.at[part], self.to_a(-k))
            self.along_b(k)
            self.share(k, 0)

    def far_a(self):
        r = self.ref(2, 0)
        self.net.wait(self.t["f", -1], r.at[self.lo])
        self.net.wait(self.t["f", 1], r.at[self.hi])
        self.along_b(2)
        self.share(2, 0)

    def near_b(self, ka):
        for k, part in ((-1, self.lo), (1, self.hi)):
            r = self.ref(ka, k)
            self.net.wait(self.t[ka, k], r)
            self.t["f", ka, k] = self.net.send(r.at[part], r.at[part], self.to_b(-k))
            self.share(ka, k)

    def far_b(self, ka):
        r = self.ref(ka, 2)
        self.net.wait(self.t["f", ka, -1], r.at[self.lo])
        self.net.wait(self.t["f", ka, 1], r.at[self.hi])
        self.share(ka, 2)


def greet(devices, extra=()):
    barrier = pltpu.get_barrier_semaphore()
    for d in devices:
        pl.semaphore_signal(barrier, inc=1, device_id=d, device_id_type=MESH)
    count = len(devices)
    for d, mine in extra:

        @pl.when(jnp.logical_not(mine))
        def _(d=d):
            pl.semaphore_signal(barrier, inc=1, device_id=d, device_id_type=MESH)

        count = count + jnp.where(mine, 0, 1)
    pl.semaphore_wait(barrier, count)


def slot_masks(rts_ref, capacity):
    r0, r1 = rts_ref[0:1, :], rts_ref[1:2, :]
    n = r0.shape[1]
    ids = lax.broadcasted_iota(jnp.int32, (8, n), 0)
    hits = ((r0 == ids) | (r1 == ids)).astype(F32).astype(BF)
    before = (
        lax.broadcasted_iota(jnp.int32, (n, n), 0)
        < lax.broadcasted_iota(jnp.int32, (n, n), 1)
    ).astype(F32).astype(BF)
    earlier = contract(hits, before, 1, 0)
    slot0 = jnp.sum(jnp.where(r0 == ids, earlier, 0.0), axis=0, keepdims=True)
    slot1 = jnp.sum(jnp.where(r1 == ids, earlier, 0.0), axis=0, keepdims=True)
    rows = lax.broadcasted_iota(jnp.int32, (capacity, n), 0)
    slot0, slot1 = slot0.astype(jnp.int32), slot1.astype(jnp.int32)
    return [
        ((r0 == e) & (slot0 == rows), (r1 == e) & (slot1 == rows)) for e in range(4)
    ]


def as_column(row):
    n = row.shape[1]
    eye = lax.broadcasted_iota(jnp.int32, (n, n), 0) == lax.broadcasted_iota(
        jnp.int32, (n, n), 1
    )
    return jnp.sum(jnp.where(eye, row, 0.0), axis=1, keepdims=True)


def layer_kernel(
    att, op, res, gain, rt, rts, cot, gate_h, up_h, down_h,
    out_h, gg_h, gu_h, gd_h,
    state_o, pr_o,
    attb, own, sib16, sibr, r1, fin, st2, tot16, projr, stat, xrow, crow, xr, cr,
    xb, wcat, wd, cb, acc, hid, sibd, sibdr, dst, dr1, dfin, dhf, dab, pcol, prow, pz, pall, yst, yr1, yfin, ysum, yvia, zs, zr,
    ssem, rsem, lsem,
):
    x, y, z, c = coords()
    h = lax.axis_index("head")
    mate = dev(x, y, z, 1 - c)
    net = Net(ssem, rsem, mate)
    turn = [(dev(2 * c + j, z, y, x // 2), (x == 2 * c + j) & (y == z) & (c == x // 2)) for j in range(2)]
    group = [
        {"expert": lax.axis_index("expert"), "head": lax.rem(h + k, 8)}
        for k in range(1, 8)
    ]
    greet(
        [dev(rot(x, k), y, z, c) for k in (1, 2, 3)]
        + [dev(x, y, rot(z, k), c) for k in (1, 2, 3)]
        + group,
        turn,
    )
    weights = [
        pltpu.make_async_copy(gate_h, wcat.at[:, :, pl.ds(0, 256)], lsem.at[1]),
        pltpu.make_async_copy(up_h, wcat.at[:, :, pl.ds(256, 256)], lsem.at[2]),
        pltpu.make_async_copy(down_h, wd, lsem.at[3]),
    ]
    for copy in weights:
        copy.start()
    attb[z, x] = att[...].reshape(attb.shape[2:])

    def quiet(ka, kb):
        pass

    def pair(ref, f):
        return jnp.concatenate(
            [ref[2 * f].astype(F32), ref[2 * f + 1].astype(F32)], axis=0
        ).astype(BF)

    def along_x(k):
        return dev(rot(x, k), y, z, c)

    def along_y(k):
        return dev(x, rot(y, k), z, c)

    lo, hi = pl.ds(0, 32), pl.ds(32, 32)
    g0 = Gather(net, lambda a, b: attb.at[b, a, 0], x, z, lambda k: dev(rot(x, k), y, z, c), lambda k: dev(x, y, rot(z, k), c), lo, hi, quiet)
    g1 = Gather(net, lambda a, b: attb.at[a, b, 1], z, x, lambda k: dev(x, y, rot(z, k), c), lambda k: dev(rot(x, k), y, z, c), lo, hi, quiet)
    flows = (g0, g1)
    for g in flows:
        g.begin()
    capacity = xrow.shape[1]
    masks = slot_masks(rts, capacity)
    for e, (m0, m1) in enumerate(masks):
        pick = (m0 | m1).astype(F32).astype(BF)
        crow[e] = contract(pick, cot[...], 1, 0).astype(BF)
    cr[z] = crow[z]
    for g in flows:
        g.near_a()
    for g in flows:
        g.near_b(0)
    for g in flows:
        g.far_a()
    for k in (-1, 1):
        for g in flows:
            g.near_b(k)
    for k in (0, -1):
        for g in flows:
            g.far_b(k)
    for g in flows:
        g.near_b(2)
    cmoved = []
    for k in (1, 2, 3):
        e = rot(z, k)
        tag = net.send(crow.at[e], cr.at[z], dev(x, y, e, c))
        cmoved.append((tag, cr.at[rot(z, -k)]))
    for k in (1, 2):
        for g in flows:
            g.far_b(k)

    def product(yy, cc):
        rows = attb[yy, pl.ds(2 * cc, 2)].reshape(256, att.shape[1])
        return contract(rows, op[...], 1, 0)

    tags = {}
    for k in (2, -1, 1, 0):
        yy = rot(y, k)
        sib16[yy] = product(yy, 1 - c).astype(BF)
        tags[k] = net.send(sib16.at[yy], sibr.at[yy], mate)
    for k in (2, -1, 1, 0):
        yy = rot(y, k)
        own[yy] = product(yy, c)
    for k in (2, -1, 1, 0):
        yy = rot(y, k)
        net.wait(tags[k], sibr.at[yy])
        own[yy] += sibr[yy].astype(F32)
        if k == 2:
            st2[0] = own[yy].astype(BF)
            ta = net.send(st2.at[0, pl.ds(0, 128)], r1.at[0], dev(x, rot(y, 1), z, c))
            tb = net.send(
                st2.at[0, pl.ds(128, 128)], r1.at[1], dev(x, rot(y, -1), z, c)
            )
    for tag, ref in cmoved:
        net.wait(tag, ref)
    for f in range(2):
        cb[f, x] = pair(cr, f)
    gc = Gather(net, lambda a, b: cb.at[:, b], x, x, along_x, along_x, pl.ds(0, 1), pl.ds(1, 1), quiet)
    gc.along_b(0)
    net.wait(ta, r1.at[0])
    yy = rot(y, 1)
    own[yy, 0:128, :] += r1[0].astype(F32)
    st2[1] = own[yy].astype(BF)
    tc = net.send(st2.at[1], fin.at[0], dev(x, yy, z, c))
    net.wait(tb, r1.at[1])
    yy = rot(y, -1)
    own[yy, 128:256, :] += r1[1].astype(F32)
    st2[2] = own[yy].astype(BF)
    td = net.send(st2.at[2], fin.at[1], dev(x, yy, z, c))
    net.wait(tc, fin.at[0])
    net.wait(td, fin.at[1])
    total = own[y] + fin[0].astype(F32) + fin[1].astype(F32)
    tot16[...] = total.reshape(tot16.shape).astype(BF)

    base = net.n
    net.n += 2
    i = x % 2
    for j, (d, mine) in enumerate(turn):

        def remote(j=j, d=d):
            return pltpu.make_async_remote_copy(
                src_ref=tot16.at[j],
                dst_ref=projr.at[i],
                send_sem=ssem.at[base + j],
                recv_sem=rsem.at[base + i],
                device_id=d,
                device_id_type=MESH,
            )

        @pl.when(mine)
        def _(j=j):
            pltpu.make_async_copy(tot16.at[j], projr.at[i], lsem.at[0]).start()

        @pl.when(jnp.logical_not(mine))
        def _(remote=remote):
            remote().start()

    gc.near_b(0)
    for k in range(2):
        local = (x == 2 * c + k) & (y == z) & (c == x // 2)

        @pl.when(local)
        def _(k=k):
            pltpu.make_async_copy(tot16.at[0], projr.at[k], lsem.at[0]).wait()

        @pl.when(jnp.logical_not(local))
        def _(k=k):
            net.wait(base + k, projr.at[k])

    for j, (d, mine) in enumerate(turn):

        @pl.when(jnp.logical_not(mine))
        def _(j=j, d=d):
            pltpu.make_async_remote_copy(
                src_ref=tot16.at[j],
                dst_ref=projr.at[i],
                send_sem=ssem.at[base + j],
                recv_sem=rsem.at[base + i],
                device_id=d,
                device_id_type=MESH,
            ).wait_send()

    half = projr.shape[2]
    for k in range(2):
        cols = slice(k * half, (k + 1) * half)
        state_o[:, cols] = res[:, cols].astype(F32) + projr[k].astype(F32)
    state = state_o[...]
    scaled = state * gain[...].astype(F32)
    stat[h, 0:4, :] = contract(rt[...], scaled, 1, 1, precision=lax.Precision.HIGHEST)
    ones = jnp.ones((8, state.shape[1]), F32)
    squares = contract(ones, state * state, 1, 1, precision=lax.Precision.HIGHEST)
    stat[h, 4:8, :] = squares[0:4]
    tags = [net.send(stat.at[h], stat.at[h], d) for d in group]
    for k, tag in enumerate(tags):
        net.wait(tag, stat.at[lax.rem(h + 7 - k, 8)])
    sums = stat[0]
    for k in range(1, 8):
        sums = sums + stat[k]
    width = 8.0 * state.shape[1]
    inverse = lax.rsqrt(sums[4:5] / width + EPSILON)
    logits = sums[0:4] * inverse
    ids = lax.broadcasted_iota(jnp.int32, logits.shape, 0)
    l0 = jnp.sum(jnp.where(rts[0:1, :] == ids, logits, 0.0), axis=0, keepdims=True)
    l1 = jnp.sum(jnp.where(rts[1:2, :] == ids, logits, 0.0), axis=0, keepdims=True)
    p0, p1 = jax.nn.sigmoid(l0 - l1), jax.nn.sigmoid(l1 - l0)
    pr_o[0:1, :] = p0
    pr_o[1:2, :] = p1
    normed = (scaled * as_column(inverse)).astype(BF)
    for e, (m0, m1) in enumerate(masks):
        pick = (m0 | m1).astype(F32).astype(BF)
        xrow[e] = contract(pick, normed, 1, 0).astype(BF)
    moved = []
    for k in (1, 2, 3):
        e = rot(z, k)
        tag = net.send(xrow.at[e], xr.at[z], dev(x, y, e, c))
        moved.append((tag, xr.at[rot(z, -k)]))
    xr[z] = xrow[z]
    both = jnp.concatenate([p0, p1, jnp.zeros((6, p0.shape[1]), F32)], axis=0)
    for e, (m0, m1) in enumerate(masks):
        first = contract(both, m0.astype(F32), 1, 1, precision=lax.Precision.HIGHEST)
        second = contract(both, m1.astype(F32), 1, 1, precision=lax.Precision.HIGHEST)
        prow[e] = jnp.zeros(prow.shape[1:], F32)
        prow[e, 0:1, 0:capacity] = first[0:1] + second[1:2]
    pmoved = []
    for k in (1, 2, 3):
        e = rot(z, k)
        tag = net.send(prow.at[e], pz.at[z], dev(x, y, e, c))
        pmoved.append((tag, pz.at[rot(z, -k)]))
    pz[z] = prow[z]
    rows, hidden = xb.shape[4], hid.shape[-1]
    for copy in weights:
        copy.wait()
    gc.far_b(0)

    def grad_hidden(yy, cc):
        c_rows = cb[...].reshape(8 * rows, cb.shape[3])
        return contract(c_rows, wd[2 * yy + cc], 1, 1).reshape(2, 4, rows, hidden)

    dtags = {}
    for k in (2, -1, 1, 0):
        yy = rot(y, k)
        sibd[yy] = grad_hidden(yy, 1 - c).astype(BF)
        dtags[k] = net.send(sibd.at[yy], sibdr.at[yy], mate)

    yy = rot(y, 2)
    net.wait(dtags[2], sibdr.at[yy])
    dst[0] = (grad_hidden(yy, c) + sibdr[yy].astype(F32)).astype(BF)
    dta = net.send(dst.at[0, 0], dr1.at[0], along_y(1))
    dtb = net.send(dst.at[0, 1], dr1.at[1], along_y(-1))
    for tag, ref in moved:
        net.wait(tag, ref)

    def sharing(at):
        tags = {}

        def share(ka, kb, at=at, tags=tags):
            r = at(ka, kb, c)
            tags[ka, kb] = net.send(r, r, mate)

        def arrived(ka, kb, at=at, tags=tags):
            net.wait(tags[ka, kb], at(ka, kb, 1 - c))

        return share, arrived

    for f in range(2):
        xb[y, c, f, x] = pair(xr, f)
    lo, hi = pl.ds(0, 80), pl.ds(80, 64)
    share0, mate0 = sharing(lambda ka, kb, cc: xb.at[rot(y, kb), cc, 0, rot(x, ka)])
    share1, mate1 = sharing(lambda ka, kb, cc: xb.at[rot(y, ka), cc, 1, rot(x, kb)])
    g0 = Gather(net, lambda a, b: xb.at[b, c, 0, a], x, y, along_x, along_y, lo, hi, share0)
    g1 = Gather(net, lambda a, b: xb.at[a, c, 1, b], y, x, along_y, along_x, lo, hi, share1)
    flows = (g0, g1)
    for g in flows:
        g.begin()
    for g in flows:
        g.near_a()
    for g in flows:
        g.near_b(0)
    for g in flows:
        g.far_a()
    for tag, ref in pmoved:
        net.wait(tag, ref)
    pall[x] = pz[...]
    ptags = []
    for k in (1, 2, 3):
        tag = net.send(pall.at[x], pall.at[x], along_x(k))
        ptags.append((tag, pall.at[rot(x, -k)]))

    def group0(kb, first):
        for ka in (0, -1, 1, 2):
            mate0(ka, kb)
        yy = rot(y, kb)
        for cc in range(2):
            part = contract(
                xb[yy, cc, 0].reshape(4 * rows, xb.shape[5]), wcat[2 * yy + cc], 1, 0
            ).reshape(4, rows, 2 * hidden)
            if first and cc == 0:
                acc[0] = part
            else:
                acc[0] += part

    def group1(kb):
        for ka in (0, -1, 1, 2):
            mate1(ka, kb)
        xx = rot(x, kb)
        total = jnp.zeros((rows, 2 * hidden), F32)
        for h2 in range(8):
            total += contract(xb[h2 // 2, h2 % 2, 1, xx], wcat[h2], 1, 0)
        acc[1, xx] = total

    for g in flows:
        g.near_b(-1)
    group0(0, True)
    for g in flows:
        g.near_b(1)
    group1(0)
    for k in (0, -1):
        for g in flows:
            g.far_b(k)
    for g in flows:
        g.near_b(2)
    for k, t, i in ((1, dta, 0), (-1, dtb, 1)):
        yy = rot(y, k)
        net.wait(dtags[k], sibdr.at[yy])
        dhf[...] = grad_hidden(yy, c) + sibdr[yy].astype(F32)
        net.wait(t, dr1.at[i])
        dhf[i] += dr1[i].astype(F32)
        dst[1 + i] = dhf[...].astype(BF)
        dtags["f", k] = net.send(dst.at[1 + i], dfin.at[i], along_y(k))
    group1(-1)
    group1(1)
    group0(-1, False)
    group0(1, False)
    for k in (1, 2):
        for g in flows:
            g.far_b(k)

    hshare, hmate = [], []
    hg = []
    for f in range(2):
        s, m = sharing(lambda ka, kb, cc, f=f: hid.at[rot(y, kb), cc, f])
        hmate.append(m)
        hg.append(Gather(net, lambda a, b, f=f: hid.at[b, c, f], y, y, along_y, along_y, pl.ds(0, 2), pl.ds(2, 2), s))
        hshare.append(s)

    def activate(f):
        a, b = acc[f, :, :, 0:hidden], acc[f, :, :, hidden : 2 * hidden]
        hid[y, c, f] = (jax.nn.silu(a) * b).astype(BF)
        hg[f].along_b(0)
        hshare[f](0, 0)

    group1(2)
    activate(1)
    group0(2, False)
    activate(0)
    net.wait(dtags[0], sibdr.at[y])
    dhf[...] = grad_hidden(y, c) + sibdr[y].astype(F32)
    for tag, ref in ptags:
        net.wait(tag, ref)
    for tag in gc.t.values():
        net.left(tag)
    for f in range(2):
        for xx in range(4):
            cols = [as_column(pall[xx, 2 * f + i, 0:1, :])[0:capacity] for i in range(2)]
            pcol[f, xx] = jnp.concatenate(cols, axis=0)
            cb[f, xx] = (cb[f, xx].astype(F32) * pcol[f, xx]).astype(BF)

    writes = []

    def write(src, dst_ref, sem):
        copy = pltpu.make_async_copy(src, dst_ref, sem)
        copy.start()
        writes.append(copy)

    def grads(h2):
        part = xb[h2 // 2, h2 % 2].reshape(8 * rows, xb.shape[5])
        wcat[h2] = contract(
            part, dab[...].reshape(8 * rows, 2 * hidden), 0, 0
        ).astype(BF)
        write(wcat.at[h2, :, pl.ds(0, hidden)], gg_h.at[h2], lsem.at[12 + h2])
        write(wcat.at[h2, :, pl.ds(hidden, hidden)], gu_h.at[h2], lsem.at[20 + h2])

    def grads_down(h2):
        part = hid[h2 // 2, h2 % 2].reshape(8 * rows, hidden)
        wd[h2] = contract(part, cb[...].reshape(8 * rows, cb.shape[3]), 0, 0).astype(BF)
        write(wd.at[h2], gd_h.at[h2], lsem.at[4 + h2])

    for i, k in ((0, 1), (1, -1)):
        net.wait(dtags["f", k], dfin.at[i])
    for f in range(2):
        dh = dhf[f] + dfin[0, f].astype(F32) + dfin[1, f].astype(F32)
        dh = dh * pcol[f]
        a, b = acc[f, :, :, 0:hidden], acc[f, :, :, hidden : 2 * hidden]
        s = jax.nn.sigmoid(a)
        dab[f, :, :, 0:hidden] = (dh * b * s * (1.0 + a * (1.0 - s))).astype(BF)
        dab[f, :, :, hidden : 2 * hidden] = (dh * (a * s)).astype(BF)
    def product_y(f, xx):
        total = jnp.zeros((rows, wd.shape[2]), F32)
        for h2 in range(8):
            total += contract(hid[h2 // 2, h2 % 2, f, xx], wd[h2], 1, 0)
        return total

    ytags = {}

    def expert_rows(f, block):
        via = 1 if f == 0 else -1
        yst[0, f] = product_y(f, rot(x, 2)).astype(BF)
        first = net.send(yst.at[0, f], yr1.at[f], along_x(via))
        yst[1, f] = product_y(f, rot(x, -via)).astype(BF)
        ytags[f, -via] = net.send(yst.at[1, f], yfin.at[1, f], along_x(-via))
        yvia[...] = product_y(f, rot(x, via))
        ysum[f] = product_y(f, x)
        grads(block)
        net.wait(first, yr1.at[f])
        yst[2, f] = (yvia[...] + yr1[f].astype(F32)).astype(BF)
        ytags[f, via] = net.send(yst.at[2, f], yfin.at[0, f], along_x(via))

    zbase = net.n
    net.n += 4

    def to_plane(zz):
        return pltpu.make_async_remote_copy(
            src_ref=zs.at[zz],
            dst_ref=zr.at[z],
            send_sem=ssem.at[zbase + zz],
            recv_sem=rsem.at[zbase + z],
            device_id=dev(x, y, zz, c),
            device_id_type=MESH,
        )

    def to_owners(f):
        via = 1 if f == 0 else -1
        net.wait(ytags[f, -via], yfin.at[1, f])
        net.wait(ytags[f, via], yfin.at[0, f])
        total = ysum[f] + yfin[0, f].astype(F32) + yfin[1, f].astype(F32)
        for i in range(2):
            zz = 2 * f + i
            zs[zz] = total[i * capacity : (i + 1) * capacity].astype(BF)

            @pl.when(z != zz)
            def _(zz=zz):
                to_plane(zz).start()

    def arrive(f):
        hg[f].far_b(0)
        for kb in (0, -1, 1, 2):
            hmate[f](0, kb)

    hg[1].near_b(0)
    grads(0)
    hg[0].near_b(0)
    for h2 in (1, 2, 3):
        grads(h2)
    arrive(1)
    expert_rows(1, 4)
    grads(5)
    arrive(0)
    expert_rows(0, 6)
    to_owners(1)
    for h2 in range(6):
        grads_down(h2)
    to_owners(0)
    for h2 in (6, 7):
        grads_down(h2)
    grads(7)
    zr[z] = zs[z]
    for k in (1, 2, 3):
        zz = rot(z, k)
        net.wait(zbase + zz, zr.at[zz])
    for zz in range(4):

        @pl.when(z != zz)
        def _(zz=zz):
            to_plane(zz).wait_send()

    took0 = jnp.zeros(state_o.shape, F32)
    took1 = jnp.zeros(state_o.shape, F32)
    for e, (m0, m1) in enumerate(slot_masks(rts, capacity)):
        took0 += contract(m0.astype(F32).astype(BF), zr[e], 0, 0)
        took1 += contract(m1.astype(F32).astype(BF), zr[e], 0, 0)
    out_h[...] = (
        state_o[...] + as_column(pr_o[0:1, :]) * took0 + as_column(pr_o[1:2, :]) * took1
    )
    for copy in writes:
        copy.wait()
    net.drain()


def shards(
    attention, out_proj, residual, norm_gain, router, routes, cotangent,
    gate_weight, up_weight, down_weight,
):
    vmem = pl.BlockSpec(memory_space=pltpu.VMEM)
    hbm = pl.BlockSpec(memory_space=pl.ANY)
    rows, cols = attention.shape
    width = out_proj.shape[1]
    cap = rows * 9 // 16
    pair_rows = 2 * cap
    hidden = gate_weight.shape[2]
    sds = jax.ShapeDtypeStruct
    layer_out, grad_gate, grad_up, grad_down = pl.pallas_call(
        layer_kernel,
        out_shape=(
            sds((rows, cols), F32),
            sds((8, cols, hidden), BF),
            sds((8, cols, hidden), BF),
            sds((8, hidden, cols), BF),
        ),
        in_specs=[vmem] * 7 + [hbm] * 3,
        out_specs=(vmem,) + (hbm,) * 3,
        scratch_shapes=[
            pltpu.VMEM((rows, cols), F32),
            pltpu.VMEM((8, rows), F32),
            pltpu.VMEM((4, 4, 2, rows // 2, cols), BF),
            pltpu.VMEM((4, 2 * rows, width), F32),
            pltpu.VMEM((4, 2 * rows, width), BF),
            pltpu.VMEM((4, 2 * rows, width), BF),
            pltpu.VMEM((2, rows, width), BF),
            pltpu.VMEM((2, 2 * rows, width), BF),
            pltpu.VMEM((3, 2 * rows, width), BF),
            pltpu.VMEM((2, rows, width), BF),
            pltpu.VMEM((2, rows, width), BF),
            pltpu.VMEM((8, 8, rows), F32),
            pltpu.VMEM((4, cap, cols), BF),
            pltpu.VMEM((4, cap, cols), BF),
            pltpu.VMEM((4, cap, cols), BF),
            pltpu.VMEM((4, cap, cols), BF),
            pltpu.VMEM((4, 2, 2, 4, pair_rows, cols), BF),
            pltpu.VMEM((8, cols, 2 * hidden), BF),
            pltpu.VMEM((8, hidden, cols), BF),
            pltpu.VMEM((2, 4, pair_rows, cols), BF),
            pltpu.VMEM((2, 4, pair_rows, 2 * hidden), F32),
            pltpu.VMEM((4, 2, 2, 4, pair_rows, hidden), BF),
            pltpu.VMEM((4, 2, 4, pair_rows, hidden), BF),
            pltpu.VMEM((4, 2, 4, pair_rows, hidden), BF),
            pltpu.VMEM((3, 2, 4, pair_rows, hidden), BF),
            pltpu.VMEM((2, 4, pair_rows, hidden), BF),
            pltpu.VMEM((2, 2, 4, pair_rows, hidden), BF),
            pltpu.VMEM((2, 4, pair_rows, hidden), F32),
            pltpu.VMEM((2, 4, pair_rows, 2 * hidden), BF),
            pltpu.VMEM((2, 4, pair_rows, 1), F32),
            pltpu.VMEM((4, 8, rows), F32),
            pltpu.VMEM((4, 8, rows), F32),
            pltpu.VMEM((4, 4, 8, rows), F32),
            pltpu.VMEM((3, 2, pair_rows, cols), BF),
            pltpu.VMEM((2, pair_rows, cols), BF),
            pltpu.VMEM((2, 2, pair_rows, cols), BF),
            pltpu.VMEM((2, pair_rows, cols), F32),
            pltpu.VMEM((pair_rows, cols), F32),
            pltpu.VMEM((4, cap, cols), BF),
            pltpu.VMEM((4, cap, cols), BF),
            pltpu.SemaphoreType.DMA((216,)),
            pltpu.SemaphoreType.DMA((216,)),
            pltpu.SemaphoreType.DMA((28,)),
        ],
        compiler_params=pltpu.CompilerParams(
            collective_id=0, has_side_effects=True, vmem_limit_bytes=63 * MIB
        ),
        cost_estimate=pl.CostEstimate(
            flops=30_000_000_000, bytes_accessed=25_000_000, transcendentals=0
        ),
    )(
        attention,
        out_proj,
        residual,
        norm_gain[None, :],
        router.T,
        routes.T,
        cotangent,
        gate_weight.reshape(8, cols, hidden),
        up_weight.reshape(8, cols, hidden),
        down_weight.reshape(8, hidden, cols),
    )
    return (
        layer_out,
        grad_gate.reshape(gate_weight.shape),
        grad_up.reshape(up_weight.shape),
        grad_down.reshape(down_weight.shape),
    )


def solution(mesh):
    token = P("expert", "head")
    weight = P("expert", None, "head")
    return jax.shard_map(
        shards,
        mesh=mesh,
        in_specs=(token, P("head", "expert"), token, P("head"), P("head", None), P("expert", None), token)
        + (weight,) * 3,
        out_specs=(token,) + (weight,) * 3,
        check_vma=False,
    )
```
